256 devices in a mesh: section: 4 (over y), seq: 16 (over z, core), tp: 4 (over x).
Axes of the slice: x: 4, y: 4, z: 8, core: 2. Of those that a mesh axis runs over, the one named last changes fastest.
Arguments:
- queries: bfloat16 [4, 6144, 4096], P('section', 'seq', 'tp'), may hold values from -6 to 6
- encoded: bfloat16 [4, 256, 128, 896], P('section', 'seq'), may hold values from -6 to 6
- neighbour: int32 [4, 96, 2], P('section', 'seq'), may hold values from 0 to 15, as said below
- send_rows: int32 [4, 16, 16, 2], P('section', 'seq'), may hold values from 0 to 15
- key_weight: bfloat16 [4, 896, 4096], P('section', None, 'tp'), may hold values from -0.1875 to 0.1875
- value_weight: bfloat16 [4, 896, 4096], P('section', None, 'tp'), may hold values from -0.1875 to 0.1875
- ctx_grad: bfloat16 [4, 6144, 4096], P('section', 'seq', 'tp'), may hold values from -6 to 6
Outputs:
- context: bfloat16 [4, 6144, 4096], P('section', 'seq', 'tp')
- passed_grad: bfloat16 [4, 6144, 4096], P('section', 'seq', 'tp')
- encoded_grad: bfloat16 [4, 256, 128, 896], P('section', 'seq', None, 'tp')
The draws below stay inside these ranges and needn't reach their ends.
Inputs may be any that keep to these rules, and one draw needn't show every extreme that they name: `neighbour`: among the 12 entries of the spans of one seq device (an aligned block of 6 spans), each device is named at most 2 times, and one device exactly 2 times. send_rows[s, i, d, j] is the row on device i of the neighbour named by the j-th entry (span order, then neighbour order) of device d's spans that names device i; slots past the number of such entries are never read.
All inputs are finite; a program needn't handle non-finite values.
Results may differ from the reference program's by a relative error of at most 0.015.
Values may be sent and summed in bfloat16 or wider, within the bound.
No kernel may reach another device: no remote copies, remote signals or barrier semaphores. Data moves between devices by JAX's collectives and lax.ppermute only.
A program may use at most 128 MiB of HBM per device.

```python
import math
import jax
import jax.numpy as jnp
from jax import lax

HEADS = 32
DH = 128
E = 896
SPAN = 64
KNB = 2
NTOK = 128
CH_DEV = 6
ENC_DEV = 16
SECTIONS = 4
SPANS = 96
TOKENS = 6144
NEIGHBOURS = 256
CAP = 2
N_SEQ = 16
N_TP = 4


def device_sources(device_key, hot_sources):
    devices = SPANS // CH_DEV
    requests = CH_DEV * KNB
    remaining = requests - CAP
    first_key, score_key, order_key = jax.random.split(device_key, 3)
    first = jax.random.randint(first_key, (), 0, devices)
    chosen_sources = jnp.full((CAP,), first, jnp.int32)
    if remaining > 0:
        tokens = jnp.arange((devices - 1) * CAP, dtype=jnp.int32)
        raw_index = tokens // CAP
        shifted = raw_index + (raw_index >= first).astype(jnp.int32)
        scores = (jax.random.randint(score_key, tokens.shape, 0, 1000) + 1000 * hot_sources[shifted]) * tokens.shape[0] + tokens
        chosen = lax.top_k(scores, remaining)[1]
        chosen_sources = jnp.concatenate([chosen_sources, shifted[chosen]])
    return chosen_sources[jax.random.permutation(order_key, requests)]


def section_sources(section_key):
    devices = SPANS // CH_DEV
    hot_sources = (jax.random.randint(jax.random.fold_in(section_key, 11), (devices,), 0, 4) == 0).astype(jnp.int32)
    device_keys = jax.random.split(section_key, devices)
    table = jax.vmap(lambda one_key: device_sources(one_key, hot_sources))(device_keys)
    return table.reshape(SPANS, KNB).astype(jnp.int32)


def draw_neighbour(key, part):
    key = jax.random.fold_in(key, 5)
    return jax.vmap(section_sources)(jax.random.split(key, SECTIONS))


def set_ends(entries, rng, smallest, largest):
    place = [jax.random.randint(jax.random.fold_in(rng, axis), (), 0, length) for axis, length in enumerate(entries.shape)]
    main_axis = entries.shape.index(max(entries.shape))
    beside = place[:main_axis] + [(place[main_axis] + 1) % entries.shape[main_axis]] + place[main_axis + 1:]
    return entries.at[tuple(place)].set(smallest).at[tuple(beside)].set(largest)


def block_scale(key, dims, shards, low, largest):
    def one(position, shards_of):
        steps = jax.random.uniform(jax.random.fold_in(jax.random.fold_in(key, 6), position), (shards_of,), jnp.float32, low / len(shards), largest / len(shards))
        return jnp.repeat(jnp.exp(steps), dims[position] // shards_of).reshape((-1,) + (1,) * (len(dims) - position - 1))

    level = one(*shards[0])
    for cut in shards[1:]:
        level = level * one(*cut)
    return level


def scatter_about(rng, dims, scale, limit, shards=(), held_as=jnp.bfloat16):
    drawn = scale * jax.random.normal(rng, dims, jnp.float32)
    if shards:
        drawn = drawn * block_scale(rng, dims, shards, -0.22, 0.18)
    return jnp.clip(drawn, -limit, limit).astype(held_as)


def setup_inputs(seed: int = 0) -> dict:
    seeds = jax.random.split(jax.random.key(seed), 8)
    queries = scatter_about(seeds[0], (SECTIONS, TOKENS, HEADS * DH), 1.0, 6.0, ((0, 4), (1, 16), (2, 4)))
    encoded = scatter_about(seeds[1], (SECTIONS, NEIGHBOURS, NTOK, E), 1.0, 6.0, ((0, 4), (1, 16)))
    neighbour = draw_neighbour(jax.random.fold_in(seeds[7], 71), 0)
    send_rows = set_ends(jax.random.randint(seeds[3], (SECTIONS, N_SEQ, N_SEQ, CAP), 0, ENC_DEV), jax.random.fold_in(seeds[3], 1), 0, ENC_DEV - 1).astype(jnp.int32)
    key_weight = scatter_about(seeds[4], (SECTIONS, E, HEADS * DH), E ** -0.5, 0.1875, ((0, 4), (2, 4)))
    value_weight = scatter_about(seeds[5], (SECTIONS, E, HEADS * DH), E ** -0.5, 0.1875, ((0, 4), (2, 4)))
    ctx_grad = scatter_about(seeds[6], (SECTIONS, TOKENS, HEADS * DH), 1.0, 6.0, ((0, 4), (1, 16), (2, 4)))
    return {"queries": queries, "encoded": encoded, "neighbour": neighbour, "send_rows": send_rows, "key_weight": key_weight, "value_weight": value_weight, "ctx_grad": ctx_grad}


def slot_ranks(sources):
    devices = sources.shape[0]
    onehot = (sources[:, :, None] == jnp.arange(devices, dtype=jnp.int32)[None, None, :]).astype(jnp.int32)
    earlier = jnp.cumsum(onehot, axis=1) - onehot
    return lax.optimization_barrier(jnp.sum(earlier * onehot, axis=2)).astype(jnp.int32)

def one_section(section_args):
    queries, encoded, neighbour, send_rows, key_weight, value_weight, ctx_grad = section_args
    devices = send_rows.shape[0]
    sources = neighbour.reshape(devices, -1).astype(jnp.int32)
    slot_index = slot_ranks(sources)
    receivers = jnp.broadcast_to(jnp.arange(devices, dtype=jnp.int32)[:, None], sources.shape)
    local_rows = send_rows[sources, receivers, slot_index].astype(jnp.int32)
    global_rows = (sources * ENC_DEV + local_rows).reshape(-1).astype(jnp.int32)
    stacked = encoded[global_rows].reshape(-1, E)
    keys_all = jnp.dot(stacked, key_weight, preferred_element_type=jnp.float32).astype(jnp.bfloat16)
    values_all = jnp.dot(stacked, value_weight, preferred_element_type=jnp.float32).astype(jnp.bfloat16)
    span_count = queries.shape[0] // SPAN
    query_blocks = queries.reshape(span_count, SPAN, HEADS, DH).astype(jnp.float32)
    key_blocks = keys_all.reshape(span_count, KNB * NTOK, HEADS, DH).astype(jnp.float32)
    value_blocks = values_all.reshape(span_count, KNB * NTOK, HEADS, DH).astype(jnp.float32)
    grad_blocks = ctx_grad.reshape(span_count, SPAN, HEADS, DH).astype(jnp.float32)
    score_scale = 1.0 / math.sqrt(DH)
    scores = jnp.einsum('cqhd,ckhd->chqk', query_blocks, key_blocks) * score_scale
    exponent = jnp.exp(scores)
    probs = exponent / lax.optimization_barrier(jnp.sum(exponent, axis=-1, keepdims=True))
    probs_low = probs.astype(jnp.bfloat16)
    context = jnp.einsum('chqk,ckhd->cqhd', probs_low.astype(jnp.float32), value_blocks).astype(jnp.bfloat16)
    prob_grad = jnp.einsum('cqhd,ckhd->chqk', grad_blocks, value_blocks)
    row_delta = lax.optimization_barrier(jnp.sum(probs * prob_grad, axis=-1, keepdims=True))
    dscore = (probs * (prob_grad - row_delta) * score_scale).astype(jnp.bfloat16).astype(jnp.float32)
    query_grad = jnp.einsum('chqk,ckhd->cqhd', dscore, key_blocks).astype(jnp.bfloat16)
    key_grad = jnp.einsum('chqk,cqhd->ckhd', dscore, query_blocks).astype(jnp.bfloat16)
    value_grad = jnp.einsum('chqk,cqhd->ckhd', probs_low.astype(jnp.float32), grad_blocks).astype(jnp.bfloat16)
    key_rows = key_grad.reshape(-1, HEADS * DH)
    value_rows = value_grad.reshape(-1, HEADS * DH)
    group_width = HEADS * DH // N_TP
    summed = jnp.zeros((key_rows.shape[0], E), jnp.float32)
    for group_index in range(N_TP):
        begin_col = group_index * group_width
        end_col = begin_col + group_width
        piece_grad = jnp.dot(key_rows[:, begin_col:end_col], key_weight[:, begin_col:end_col].T, preferred_element_type=jnp.float32)
        piece_grad = piece_grad + jnp.dot(value_rows[:, begin_col:end_col], value_weight[:, begin_col:end_col].T, preferred_element_type=jnp.float32)
        rounded = lax.optimization_barrier(piece_grad.astype(jnp.bfloat16))
        summed = summed + rounded.astype(jnp.float32)
    row_grad = summed.astype(jnp.bfloat16).reshape(global_rows.shape[0], -1)
    encoded_grad = jax.ops.segment_sum(row_grad.astype(jnp.float32), global_rows, num_segments=encoded.shape[0])
    encoded_grad = encoded_grad.reshape(encoded.shape).astype(jnp.bfloat16)
    return (context.reshape(queries.shape), query_grad.reshape(queries.shape), encoded_grad)

def reference(queries, encoded, neighbour, send_rows, key_weight, value_weight, ctx_grad):
    context, query_grad, encoded_grad = lax.map(one_section, (queries, encoded, neighbour, send_rows, key_weight, value_weight, ctx_grad))
    passed_grad = jnp.concatenate([query_grad[1:], jnp.zeros_like(query_grad[:1])], axis=0)
    return (context, passed_grad, encoded_grad)
```

```python
import math

import jax
import jax.numpy as jnp
from jax import lax
from jax.experimental import pallas as pl
from jax.experimental.pallas import tpu as pltpu
from jax.sharding import PartitionSpec as P

DH = 128
E = 896
SPAN = 64
KNB = 2
NTOK = 128
N_SEQ = 16
CHIPS = N_SEQ // 2
CAP = 2
N_TP = 4
SLOTS = N_SEQ * CAP
REQ = 12
STORED = 16
SPANS_DEV = 6
TOKENS_DEV = SPANS_DEV * SPAN
HEADS_DEV = 8
WIDTH = HEADS_DEV * DH
PART = NTOK // N_TP
EQ = E // N_TP
KEYS = KNB * NTOK
GROUPS = ((0, 3), (3, 3))
VMEM = 24 * 1024 * 1024
WIDE_VMEM = 60 * 1024 * 1024
BF16 = jnp.bfloat16
F32 = jnp.float32
SCALE = 1.0 / math.sqrt(DH)
IN_SMEM = pl.BlockSpec(memory_space=pltpu.SMEM)
IN_VMEM = pl.BlockSpec(memory_space=pltpu.VMEM)
ANYWHERE = pl.BlockSpec(memory_space=pl.ANY)


def params(limit=VMEM):
    return pltpu.CompilerParams(vmem_limit_bytes=limit)


def cost(flops, bytes_accessed):
    return pl.CostEstimate(flops=flops, bytes_accessed=bytes_accessed, transcendentals=0)


def dot(a, b):
    return jnp.dot(a, b, preferred_element_type=F32)


def dot_nt(a, b):
    return lax.dot_general(a, b, (((1,), (1,)), ((), ())), preferred_element_type=F32)


def dot_tn(a, b):
    return lax.dot_general(a, b, (((0,), (0,)), ((), ())), preferred_element_type=F32)


def member(shift):
    return lax.rem(lax.axis_index("tp") + shift, N_TP)


def share_kernel(encoded_ref, out_ref, sem):
    start = pl.multiple_of(lax.axis_index("tp") * PART, PART)
    copy = pltpu.make_async_copy(encoded_ref.at[:, pl.ds(start, PART)], out_ref, sem)
    copy.start()
    copy.wait()


def take_share(encoded):
    return pl.pallas_call(
        share_kernel,
        out_shape=jax.ShapeDtypeStruct((STORED, PART, E), BF16),
        in_specs=[ANYWHERE],
        out_specs=IN_VMEM,
        scratch_shapes=[pltpu.SemaphoreType.DMA],
        compiler_params=params(WIDE_VMEM),
        cost_estimate=cost(0, 2_000_000),
        name="take_share",
    )(encoded)


def pack_kernel(rows_ref, sibling_rows_ref, share_ref, sibling_ref, *outs):
    me = lax.axis_index("seq")
    chip, core = me // 2, lax.rem(me, 2)
    for ahead in range(CHIPS):
        device = lax.rem(chip + ahead, CHIPS) * 2 + core
        for j in range(CAP):
            row = jnp.clip(rows_ref[device, j], 0, STORED - 1)
            outs[ahead][j] = share_ref[row]
            row = jnp.clip(sibling_rows_ref[device, j], 0, STORED - 1)
            outs[ahead][CAP + j] = sibling_ref[row]


def pack_rows(rows, sibling_rows, share, sibling):
    return pl.pallas_call(
        pack_kernel,
        out_shape=[jax.ShapeDtypeStruct((2 * CAP, PART, E), BF16)] * CHIPS,
        in_specs=[IN_SMEM, IN_SMEM, IN_VMEM, IN_VMEM],
        out_specs=[IN_VMEM] * CHIPS,
        compiler_params=params(WIDE_VMEM),
        cost_estimate=cost(0, 3_000_000),
        name="pack_rows",
    )(rows, sibling_rows, share, sibling)


def places_of(neighbour_ref):
    me = lax.axis_index("seq")
    chip, core = me // 2, lax.rem(me, 2)
    sources = [neighbour_ref[r // KNB, r % KNB] for r in range(REQ)]
    places = []
    for r in range(REQ):
        earlier = jnp.int32(0)
        for q in range(r):
            earlier = earlier + (sources[q] == sources[r]).astype(jnp.int32)
        away = lax.rem(sources[r] // 2 - chip + CHIPS, CHIPS)
        other = (lax.rem(sources[r], 2) != core).astype(jnp.int32)
        places.append((away, other, jnp.minimum(earlier, CAP - 1)))
    return places


def pick_kernel(neighbour_ref, *refs):
    arrived, outs, table = refs[:CHIPS], refs[CHIPS:-1], refs[-1]
    for at in range(SLOTS):
        table[at] = REQ
    for r, (away, other, slot) in enumerate(places_of(neighbour_ref)):
        table[away * 2 * CAP + other * CAP + slot] = r
    half = GROUPS[0][1] * KNB
    for away in range(CHIPS):
        for block in range(2 * CAP):
            r = table[away * 2 * CAP + block]
            ref = arrived[(CHIPS - away) % CHIPS]

            @pl.when(r < half)
            def _():
                outs[0][r] = ref[block]

            @pl.when((r >= half) & (r < REQ))
            def _():
                outs[1][r - half] = ref[block]


def pick(neighbour, arrived):
    return pl.pallas_call(
        pick_kernel,
        out_shape=[
            jax.ShapeDtypeStruct((spans * KNB, PART, E), BF16) for first, spans in GROUPS
        ],
        in_specs=[IN_SMEM] + [IN_VMEM] * CHIPS,
        out_specs=[IN_VMEM] * len(GROUPS),
        scratch_shapes=[pltpu.SMEM((SLOTS,), jnp.int32)],
        compiler_params=params(),
        cost_estimate=cost(0, 3_000_000),
        name="pick",
    )(neighbour, *arrived)


def attention_kernel(*refs):
    pieces = refs[:N_TP]
    kw_ref, vw_ref, q_ref, g_ref = refs[N_TP : N_TP + 4]
    ctx_ref, qg_ref = refs[-(N_TP + 7) : -(N_TP + 5)]
    outs = refs[-(N_TP + 5) : -5]
    xs, ks, vs, kgs, vgs = refs[-5:]
    for shift in range(N_TP):
        begin = pl.multiple_of(member(shift) * PART, PART)
        for k in range(KNB):
            xs[k, pl.ds(begin, PART), :] = pieces[shift][k]
    x = xs[...].reshape(KEYS, E)
    ks[...] = dot(x, kw_ref[...]).astype(BF16)
    vs[...] = dot(x, vw_ref[...]).astype(BF16)
    cols = [slice(h * DH, (h + 1) * DH) for h in range(HEADS_DEV)]
    scores = [dot_nt(q_ref[:, c], ks[:, c]) for c in cols]
    prob_grads = [dot_nt(g_ref[:, c], vs[:, c]) for c in cols]
    lows, dscores = [], []
    for score, prob_grad in zip(scores, prob_grads):
        exponent = jnp.exp(score * SCALE)
        probs = exponent / jnp.sum(exponent, axis=-1, keepdims=True)
        delta = jnp.sum(probs * prob_grad, axis=-1, keepdims=True)
        lows.append(probs.astype(BF16))
        dscores.append((probs * (prob_grad - delta) * SCALE).astype(BF16))
    for c, low, dscore in zip(cols, lows, dscores):
        kgs[c, :] = dot_tn(q_ref[:, c], dscore).astype(BF16)
        vgs[c, :] = dot_tn(g_ref[:, c], low).astype(BF16)
    for c, low, dscore in zip(cols, lows, dscores):
        ctx_ref[:, c] = dot(low, vs[:, c]).astype(BF16)
        qg_ref[:, c] = dot(dscore, ks[:, c]).astype(BF16)
    for shift in range(N_TP):
        begin = pl.multiple_of(member(shift) * EQ, 16)
        piece = dot(kw_ref[pl.ds(begin, EQ), :], kgs[...])
        piece = (piece + dot(vw_ref[pl.ds(begin, EQ), :], vgs[...])).astype(BF16)
        for k in range(KNB):
            outs[shift][k] = piece[:, k * NTOK : (k + 1) * NTOK]


def attention(pieces, kw, vw, queries, ctx_grad, first, spans, held):
    whole = pl.BlockSpec((E, WIDTH), lambda c: (0, 0))
    span = pl.BlockSpec((SPAN, WIDTH), lambda c: (c + first, 0))
    arrived = pl.BlockSpec((KNB, PART, E), lambda c: (c, 0, 0))
    back = pl.BlockSpec((KNB, EQ, NTOK), lambda c: (c, 0, 0))
    wide = jax.ShapeDtypeStruct((TOKENS_DEV, WIDTH), BF16)
    piece = jax.ShapeDtypeStruct((spans * KNB, EQ, NTOK), BF16)
    at = N_TP + 4
    return pl.pallas_call(
        attention_kernel,
        grid=(spans,),
        out_shape=[wide, wide] + [piece] * N_TP,
        in_specs=[arrived] * N_TP + [whole, whole, span, span] + [ANYWHERE] * len(held),
        out_specs=[span, span] + [back] * N_TP,
        scratch_shapes=[
            pltpu.VMEM((KNB, NTOK, E), BF16),
            pltpu.VMEM((KEYS, WIDTH), BF16),
            pltpu.VMEM((KEYS, WIDTH), BF16),
            pltpu.VMEM((WIDTH, KEYS), BF16),
            pltpu.VMEM((WIDTH, KEYS), BF16),
        ],
        input_output_aliases={at + i: i for i in range(len(held))},
        compiler_params=params(),
        cost_estimate=cost(spans * 2_200_000_000, 5_000_000 + spans * 1_500_000),
        name="attention",
    )(*pieces, kw, vw, queries, ctx_grad, *held)


def sum_kernel(*refs):
    out_ref = refs[-1]
    for r in range(out_ref.shape[0]):
        total = refs[0][r].astype(F32)
        for part in refs[1:-1]:
            total = total + part[r].astype(F32)
        out_ref[r] = total.astype(BF16)


def sum_parts(parts):
    return pl.pallas_call(
        sum_kernel,
        out_shape=jax.ShapeDtypeStruct(parts[0].shape, BF16),
        in_specs=[IN_VMEM] * len(parts),
        out_specs=IN_VMEM,
        compiler_params=params(),
        cost_estimate=cost(0, 2_000_000),
        name="sum_parts",
    )(*parts)


def place_kernel(neighbour_ref, sibling_neighbour_ref, *refs):
    grads, outs, table = refs[:4], refs[4:-1], refs[-1]
    half = GROUPS[0][1] * KNB
    for at in range(SLOTS):
        table[at] = REQ
    for whose, ref in enumerate((neighbour_ref, sibling_neighbour_ref)):
        for r, (away, other, slot) in enumerate(places_of(ref)):
            at = away * 2 * CAP + whose * CAP + slot

            @pl.when(other == 0)
            def _():
                table[at] = r

    for away in range(CHIPS):
        for block in range(2 * CAP):
            r = table[away * 2 * CAP + block]
            low, high = grads[2 * (block // CAP)], grads[2 * (block // CAP) + 1]
            out = outs[away]

            @pl.when(r < half)
            def _():
                out[block] = low[r]

            @pl.when((r >= half) & (r < REQ))
            def _():
                out[block] = high[r - half]

            @pl.when(r >= REQ)
            def _():
                out[block] = jnp.zeros((EQ, NTOK), BF16)


def place(neighbour, sibling_neighbour, grads):
    return pl.pallas_call(
        place_kernel,
        out_shape=[jax.ShapeDtypeStruct((2 * CAP, EQ, NTOK), BF16)] * CHIPS,
        in_specs=[IN_SMEM, IN_SMEM] + [IN_VMEM] * len(grads),
        out_specs=[IN_VMEM] * CHIPS,
        scratch_shapes=[pltpu.SMEM((SLOTS,), jnp.int32)],
        compiler_params=params(),
        cost_estimate=cost(0, 3_000_000),
        name="place",
    )(neighbour, sibling_neighbour, *grads)


def collect_kernel(rows_ref, *refs):
    arrived, (out_ref, acc) = refs[:CHIPS], refs[CHIPS:]
    me = lax.axis_index("seq")
    chip, core = me // 2, lax.rem(me, 2)
    acc[...] = jnp.zeros(acc.shape, F32)
    for behind in range(CHIPS):
        device = lax.rem(chip - behind + CHIPS, CHIPS) * 2
        for block in range(2 * CAP):
            requester = device + (core if block < CAP else 1 - core)
            row = jnp.clip(rows_ref[requester, block % CAP], 0, STORED - 1)
            acc[row] += arrived[behind][block].astype(F32)
    out_ref[...] = acc[...].astype(BF16)


def collect(rows, arrived):
    return pl.pallas_call(
        collect_kernel,
        out_shape=jax.ShapeDtypeStruct((STORED, EQ, NTOK), BF16),
        in_specs=[IN_SMEM] + [IN_VMEM] * CHIPS,
        out_specs=IN_VMEM,
        scratch_shapes=[pltpu.VMEM((STORED, EQ, NTOK), F32)],
        compiler_params=params(),
        cost_estimate=cost(0, 3_000_000),
        name="collect",
    )(rows, *arrived)


def swap(x):
    return lax.ppermute(x, "seq", [(i, i ^ 1) for i in range(N_SEQ)])


def ahead(x, by):
    return lax.ppermute(x, "seq", [(i, (i + 2 * by) % N_SEQ) for i in range(N_SEQ)])


def after(x, *done):
    return lax.optimization_barrier((x,) + done)[0]


def exchange(messages):
    arrived = [messages[0]] + [None] * (CHIPS - 1)
    for by, behind in ((3, 0), (5, 0), (4, 0), (2, 0), (6, 0), (1, 3), (7, 5)):
        message = messages[by]
        if behind:
            message = after(message, arrived[behind])
        arrived[by] = ahead(message, by)
    return arrived


def turn(x, by):
    return lax.ppermute(x, "tp", [(i, (i + by) % N_TP) for i in range(N_TP)])


def section_back(x):
    count = lax.axis_size("section")
    return lax.ppermute(x, "section", [(i, i - 1) for i in range(1, count)])


def deliver_kernel(*refs):
    out_ref = refs[-1]
    at = 0
    for ref in refs[:-1]:
        rows = ref.shape[0]
        out_ref[at : at + rows] = ref[...]
        at += rows


def deliver(parts):
    return pl.pallas_call(
        deliver_kernel,
        out_shape=jax.ShapeDtypeStruct((TOKENS_DEV, WIDTH), BF16),
        in_specs=[IN_VMEM] * len(parts),
        out_specs=IN_VMEM,
        compiler_params=params(),
        cost_estimate=cost(0, 2_000_000),
        name="deliver",
    )(*parts)


def body(queries, encoded, neighbour, send_rows, key_weight, value_weight, ctx_grad):
    sources, rows = neighbour[0], send_rows[0, 0]
    kw, vw = key_weight[0], value_weight[0]
    share = take_share(encoded[0])
    sibling_sources = swap(sources)
    sibling_rows = after(swap(rows), sibling_sources)
    arrived = exchange(pack_rows(rows, sibling_rows, share, swap(share)))
    picked = pick(sources, arrived)
    whole = []
    for own in picked:
        if whole:
            own = after(own, whole[0][-1])
        whole.append([own] + [turn(own, -shift) for shift in range(1, N_TP)])
    held = ()
    grads = []
    for group, (first, spans) in enumerate(GROUPS):
        *held, first_piece, second, third, fourth = attention(
            whole[group], kw, vw, queries[0], ctx_grad[0], first, spans, held
        )
        turned = [turn(x, by) for by, x in ((1, second), (2, third), (3, fourth))]
        grads.append(sum_parts([first_piece] + turned))
    context, query_grad = held
    passed = section_back(query_grad)
    messages = place(sources, sibling_sources, grads + [swap(grad) for grad in grads])
    returned = exchange(messages)
    encoded_grad = jnp.swapaxes(collect(rows, returned), 1, 2)
    passed = deliver([after(passed, returned[3])])
    return (context[None], passed[None], encoded_grad[None])


def solution(mesh):
    placed = (
        P("section", "seq", "tp"),
        P("section", "seq", None, None),
        P("section", "seq", None),
        P("section", "seq", None, None),
        P("section", None, "tp"),
        P("section", None, "tp"),
        P("section", "seq", "tp"),
    )
    return jax.shard_map(
        body,
        mesh=mesh,
        in_specs=placed,
        out_specs=(
            P("section", "seq", "tp"),
            P("section", "seq", "tp"),
            P("section", "seq", None, "tp"),
        ),
        check_vma=False,
    )
```

```python
import math

import jax
import jax.numpy as jnp
from jax import lax
from jax.experimental import pallas as pl
from jax.experimental.pallas import tpu as pltpu
from jax.sharding import PartitionSpec as P

DH = 128
E = 896
SPAN = 64
KNB = 2
NTOK = 128
N_SEQ = 16
CHIPS = N_SEQ // 2
CAP = 2
N_TP = 4
SLOTS = N_SEQ * CAP
REQ = 12
STORED = 16
SPANS_DEV = 6
TOKENS_DEV = SPANS_DEV * SPAN
HEADS_DEV = 8
WIDTH = HEADS_DEV * DH
PART = NTOK // N_TP
EQ = E // N_TP
KEYS = KNB * NTOK
GROUPS = ((0, 3), (3, 3))
VMEM = 16 * 1024 * 1024
WIDE_VMEM = 60 * 1024 * 1024
STREAMS = 4
FAR = (0, 3, 5, 4, 2)
NEAR = (6, 1, 7)
BF16 = jnp.bfloat16
F32 = jnp.float32
SCALE = 1.0 / math.sqrt(DH)
IN_SMEM = pl.BlockSpec(memory_space=pltpu.SMEM)
IN_VMEM = pl.BlockSpec(memory_space=pltpu.VMEM)
ANYWHERE = pl.BlockSpec(memory_space=pl.ANY)


def params(limit=VMEM):
    return pltpu.CompilerParams(vmem_limit_bytes=limit)


def cost(flops, bytes_accessed):
    return pl.CostEstimate(flops=flops, bytes_accessed=bytes_accessed, transcendentals=0)


def dot(a, b):
    return jnp.dot(a, b, preferred_element_type=F32)


def dot_nt(a, b):
    return lax.dot_general(a, b, (((1,), (1,)), ((), ())), preferred_element_type=F32)


def dot_tn(a, b):
    return lax.dot_general(a, b, (((0,), (0,)), ((), ())), preferred_element_type=F32)


def member(shift):
    return lax.rem(lax.axis_index("tp") + shift, N_TP)


def share_kernel(encoded_ref, out_ref, buffer, in_sems, out_sems):
    start = pl.multiple_of(lax.axis_index("tp") * PART, PART)
    reads, writes = [], []
    for n in range(STREAMS):
        rows = pl.ds(n * (STORED // STREAMS), STORED // STREAMS)
        source = encoded_ref.at[rows, pl.ds(start, PART)]
        reads.append(pltpu.make_async_copy(source, buffer.at[rows], in_sems.at[n]))
        writes.append(pltpu.make_async_copy(buffer.at[rows], out_ref.at[rows], out_sems.at[n]))
    for read in reads:
        read.start()
    for read, write in zip(reads, writes):
        read.wait()
        write.start()
    for write in writes:
        write.wait()


def take_share(encoded):
    return pl.pallas_call(
        share_kernel,
        out_shape=jax.ShapeDtypeStruct((STORED, PART, E), BF16),
        in_specs=[ANYWHERE],
        out_specs=ANYWHERE,
        scratch_shapes=[
            pltpu.VMEM((STORED, PART, E), BF16),
            pltpu.SemaphoreType.DMA((STREAMS,)),
            pltpu.SemaphoreType.DMA((STREAMS,)),
        ],
        compiler_params=params(WIDE_VMEM),
        cost_estimate=cost(0, 2_000_000),
        name="take_share",
    )(encoded)


def pack_kernel(rows_ref, sibling_rows_ref, share_ref, sibling_ref, *refs):
    outs, (held, messages, in_sems, out_sems) = refs[:CHIPS], refs[CHIPS:]
    reads = [
        pltpu.make_async_copy(ref, held.at[whose], in_sems.at[whose])
        for whose, ref in enumerate((share_ref, sibling_ref))
    ]
    for read in reads:
        read.start()
    for read in reads:
        read.wait()
    me = lax.axis_index("seq")
    chip, core = me // 2, lax.rem(me, 2)
    writes = []
    for by in (3, 5, 4, 2, 6, 1, 7, 0):
        device = lax.rem(chip + by, CHIPS) * 2 + core
        for whose, table in enumerate((rows_ref, sibling_rows_ref)):
            for j in range(CAP):
                row = jnp.clip(table[device, j], 0, STORED - 1)
                messages[by, whose * CAP + j] = held[whose, row]
        writes.append(pltpu.make_async_copy(messages.at[by], outs[by], out_sems.at[by]))
        writes[-1].start()
    for write in writes:
        write.wait()


def pack_rows(rows, sibling_rows, share, sibling):
    return pl.pallas_call(
        pack_kernel,
        out_shape=[jax.ShapeDtypeStruct((2 * CAP, PART, E), BF16)] * CHIPS,
        in_specs=[IN_SMEM, IN_SMEM, ANYWHERE, ANYWHERE],
        out_specs=[ANYWHERE] * CHIPS,
        scratch_shapes=[
            pltpu.VMEM((2, STORED, PART, E), BF16),
            pltpu.VMEM((CHIPS, 2 * CAP, PART, E), BF16),
            pltpu.SemaphoreType.DMA((2,)),
            pltpu.SemaphoreType.DMA((CHIPS,)),
        ],
        compiler_params=params(WIDE_VMEM),
        cost_estimate=cost(0, 3_000_000),
        name="pack_rows",
    )(rows, sibling_rows, share, sibling)


def places_of(neighbour_ref):
    me = lax.axis_index("seq")
    chip, core = me // 2, lax.rem(me, 2)
    sources = [neighbour_ref[r // KNB, r % KNB] for r in range(REQ)]
    places = []
    for r in range(REQ):
        earlier = jnp.int32(0)
        for q in range(r):
            earlier = earlier + (sources[q] == sources[r]).astype(jnp.int32)
        away = lax.rem(sources[r] // 2 - chip + CHIPS, CHIPS)
        other = (lax.rem(sources[r], 2) != core).astype(jnp.int32)
        places.append((away, other, jnp.minimum(earlier, CAP - 1)))
    return places


def pick_kernel(neighbour_ref, *refs):
    arrived, outs, (table, local, sem) = refs[:CHIPS], refs[CHIPS:-3], refs[-3:]
    copy = pltpu.make_async_copy(arrived[0], local, sem)
    copy.start()
    for at in range(SLOTS):
        table[at] = REQ
    for r, (away, other, slot) in enumerate(places_of(neighbour_ref)):
        table[away * 2 * CAP + other * CAP + slot] = r
    half = GROUPS[0][1] * KNB
    for away in (1, 2, 3, 4, 5, 6, 7, 0):
        if away == 0:
            copy.wait()
        for block in range(2 * CAP):
            r = table[away * 2 * CAP + block]
            ref = arrived[CHIPS - away] if away else local

            @pl.when(r < half)
            def _():
                outs[0][r] = ref[block]

            @pl.when((r >= half) & (r < REQ))
            def _():
                outs[1][r - half] = ref[block]


def pick(neighbour, arrived):
    return pl.pallas_call(
        pick_kernel,
        out_shape=[
            jax.ShapeDtypeStruct((spans * KNB, PART, E), BF16) for first, spans in GROUPS
        ],
        in_specs=[IN_SMEM, ANYWHERE] + [IN_VMEM] * (CHIPS - 1),
        out_specs=[IN_VMEM] * len(GROUPS),
        scratch_shapes=[
            pltpu.SMEM((SLOTS,), jnp.int32),
            pltpu.VMEM((2 * CAP, PART, E), BF16),
            pltpu.SemaphoreType.DMA,
        ],
        compiler_params=params(),
        cost_estimate=cost(0, 3_000_000),
        name="pick",
    )(neighbour, *arrived)


def attention_kernel(*refs):
    pieces = refs[:N_TP]
    kw_ref, vw_ref, q_ref, g_ref = refs[N_TP : N_TP + 4]
    ctx_ref, qg_ref = refs[-(N_TP + 7) : -(N_TP + 5)]
    outs = refs[-(N_TP + 5) : -5]
    xs, ks, vs, kgs, vgs = refs[-5:]
    for shift in range(N_TP):
        begin = pl.multiple_of(member(shift) * PART, PART)
        for k in range(KNB):
            xs[k, pl.ds(begin, PART), :] = pieces[shift][k]
    x = xs[...].reshape(KEYS, E)
    ks[...] = dot(x, kw_ref[...]).astype(BF16)
    vs[...] = dot(x, vw_ref[...]).astype(BF16)
    cols = [slice(h * DH, (h + 1) * DH) for h in range(HEADS_DEV)]
    scores = [dot_nt(q_ref[:, c], ks[:, c]) for c in cols]
    prob_grads = [dot_nt(g_ref[:, c], vs[:, c]) for c in cols]
    lows, dscores = [], []
    for score, prob_grad in zip(scores, prob_grads):
        exponent = jnp.exp(score * SCALE)
        probs = exponent / jnp.sum(exponent, axis=-1, keepdims=True)
        delta = jnp.sum(probs * prob_grad, axis=-1, keepdims=True)
        lows.append(probs.astype(BF16))
        dscores.append((probs * (prob_grad - delta) * SCALE).astype(BF16))
    for c, low, dscore in zip(cols, lows, dscores):
        kgs[c, :] = dot_tn(q_ref[:, c], dscore).astype(BF16)
        vgs[c, :] = dot_tn(g_ref[:, c], low).astype(BF16)
    for c, low, dscore in zip(cols, lows, dscores):
        ctx_ref[:, c] = dot(low, vs[:, c]).astype(BF16)
        qg_ref[:, c] = dot(dscore, ks[:, c]).astype(BF16)
    for shift in range(N_TP):
        begin = pl.multiple_of(member(shift) * EQ, 16)
        piece = dot(kw_ref[pl.ds(begin, EQ), :], kgs[...])
        piece = (piece + dot(vw_ref[pl.ds(begin, EQ), :], vgs[...])).astype(BF16)
        for k in range(KNB):
            outs[shift][k] = piece[:, k * NTOK : (k + 1) * NTOK]


def attention(pieces, kw, vw, queries, ctx_grad, first, spans, held):
    whole = pl.BlockSpec((E, WIDTH), lambda c: (0, 0))
    span = pl.BlockSpec((SPAN, WIDTH), lambda c: (c + first, 0))
    arrived = pl.BlockSpec((KNB, PART, E), lambda c: (c, 0, 0))
    back = pl.BlockSpec((KNB, EQ, NTOK), lambda c: (c, 0, 0))
    wide = jax.ShapeDtypeStruct((TOKENS_DEV, WIDTH), BF16)
    piece = jax.ShapeDtypeStruct((spans * KNB, EQ, NTOK), BF16)
    at = N_TP + 4
    return pl.pallas_call(
        attention_kernel,
        grid=(spans,),
        out_shape=[wide, wide] + [piece] * N_TP,
        in_specs=[arrived] * N_TP + [whole, whole, span, span] + [ANYWHERE] * len(held),
        out_specs=[span, span] + [back] * N_TP,
        scratch_shapes=[
            pltpu.VMEM((KNB, NTOK, E), BF16),
            pltpu.VMEM((KEYS, WIDTH), BF16),
            pltpu.VMEM((KEYS, WIDTH), BF16),
            pltpu.VMEM((WIDTH, KEYS), BF16),
            pltpu.VMEM((WIDTH, KEYS), BF16),
        ],
        input_output_aliases={at + i: i for i in range(len(held))},
        compiler_params=params(),
        cost_estimate=cost(spans * 2_200_000_000, 5_000_000 + spans * 1_500_000),
        name="attention",
    )(*pieces, kw, vw, queries, ctx_grad, *held)


def sum_kernel(*refs):
    out_ref = refs[-1]
    for r in range(out_ref.shape[0]):
        total = refs[0][r].astype(F32)
        for part in refs[1:-1]:
            total = total + part[r].astype(F32)
        out_ref[r] = total.astype(BF16)


def sum_parts(parts):
    return pl.pallas_call(
        sum_kernel,
        out_shape=jax.ShapeDtypeStruct(parts[0].shape, BF16),
        in_specs=[IN_VMEM] * len(parts),
        out_specs=IN_VMEM,
        compiler_params=params(),
        cost_estimate=cost(0, 2_000_000),
        name="sum_parts",
    )(*parts)


def place_kernel(neighbour_ref, sibling_neighbour_ref, *refs):
    grads, outs, table = refs[:4], refs[4:-1], refs[-1]
    half = GROUPS[0][1] * KNB
    for at in range(SLOTS):
        table[at] = REQ
    for whose, ref in enumerate((neighbour_ref, sibling_neighbour_ref)):
        for r, (away, other, slot) in enumerate(places_of(ref)):
            at = away * 2 * CAP + whose * CAP + slot

            @pl.when(other == 0)
            def _():
                table[at] = r

    for away in range(CHIPS):
        for block in range(2 * CAP):
            r = table[away * 2 * CAP + block]
            low, high = grads[2 * (block // CAP)], grads[2 * (block // CAP) + 1]
            out = outs[away]

            @pl.when(r < half)
            def _():
                out[block] = low[r]

            @pl.when((r >= half) & (r < REQ))
            def _():
                out[block] = high[r - half]

            @pl.when(r >= REQ)
            def _():
                out[block] = jnp.zeros((EQ, NTOK), BF16)


def place(neighbour, sibling_neighbour, grads):
    return pl.pallas_call(
        place_kernel,
        out_shape=[jax.ShapeDtypeStruct((2 * CAP, EQ, NTOK), BF16)] * CHIPS,
        in_specs=[IN_SMEM, IN_SMEM] + [IN_VMEM] * len(grads),
        out_specs=[IN_VMEM] * CHIPS,
        scratch_shapes=[pltpu.SMEM((SLOTS,), jnp.int32)],
        compiler_params=params(),
        cost_estimate=cost(0, 3_000_000),
        name="place",
    )(neighbour, sibling_neighbour, *grads)


def add_arrived(rows_ref, arrived, acc):
    me = lax.axis_index("seq")
    chip, core = me // 2, lax.rem(me, 2)
    for behind, ref in arrived:
        device = lax.rem(chip - behind + CHIPS, CHIPS) * 2
        for block in range(2 * CAP):
            requester = device + (core if block < CAP else 1 - core)
            row = jnp.clip(rows_ref[requester, block % CAP], 0, STORED - 1)
            acc[row] += ref[block].astype(F32)


def collect_far_kernel(rows_ref, *refs):
    acc = refs[-1]
    acc[...] = jnp.zeros(acc.shape, F32)
    add_arrived(rows_ref, list(zip(FAR, refs[:-1])), acc)


def collect_near_kernel(rows_ref, acc, *refs):
    add_arrived(rows_ref, list(zip(NEAR, refs[:-1])), acc)
    refs[-1][...] = acc[...].astype(BF16)


def collect(rows, arrived):
    shape = (STORED, EQ, NTOK)
    far = pl.pallas_call(
        collect_far_kernel,
        out_shape=jax.ShapeDtypeStruct(shape, F32),
        in_specs=[IN_SMEM] + [IN_VMEM] * len(FAR),
        out_specs=IN_VMEM,
        compiler_params=params(),
        cost_estimate=cost(0, 5_000_000),
        name="collect_far",
    )(rows, *[arrived[by] for by in FAR])
    return pl.pallas_call(
        collect_near_kernel,
        out_shape=jax.ShapeDtypeStruct(shape, BF16),
        in_specs=[IN_SMEM] + [IN_VMEM] * (1 + len(NEAR)),
        out_specs=IN_VMEM,
        compiler_params=params(),
        cost_estimate=cost(0, 5_000_000),
        name="collect_near",
    )(rows, far, *[arrived[by] for by in NEAR])


def swap(x):
    return lax.ppermute(x, "seq", [(i, i ^ 1) for i in range(N_SEQ)])


def ahead(x, by):
    return lax.ppermute(x, "seq", [(i, (i + 2 * by) % N_SEQ) for i in range(N_SEQ)])


def after(x, *done):
    return lax.optimization_barrier((x,) + done)[0]


def exchange(messages):
    arrived = [messages[0]] + [None] * (CHIPS - 1)
    for by, behind in ((3, 0), (5, 0), (4, 0), (2, 0), (6, 0), (1, 3), (7, 5)):
        message = messages[by]
        if behind:
            message = after(message, arrived[behind])
        arrived[by] = ahead(message, by)
    return arrived


def turn(x, by):
    return lax.ppermute(x, "tp", [(i, (i + by) % N_TP) for i in range(N_TP)])


def section_back(x):
    count = lax.axis_size("section")
    return lax.ppermute(x, "section", [(i, i - 1) for i in range(1, count)])


def deliver_kernel(*refs):
    out_ref = refs[-1]
    at = 0
    for ref in refs[:-1]:
        rows = ref.shape[0]
        out_ref[at : at + rows] = ref[...]
        at += rows


def deliver(parts):
    return pl.pallas_call(
        deliver_kernel,
        out_shape=jax.ShapeDtypeStruct((TOKENS_DEV, WIDTH), BF16),
        in_specs=[IN_VMEM] * len(parts),
        out_specs=IN_VMEM,
        compiler_params=params(),
        cost_estimate=cost(0, 2_000_000),
        name="deliver",
    )(*parts)


def body(queries, encoded, neighbour, send_rows, key_weight, value_weight, ctx_grad):
    sources, rows = neighbour[0], send_rows[0, 0]
    kw, vw = key_weight[0], value_weight[0]
    share = take_share(encoded[0])
    sibling_sources = swap(sources)
    sibling_rows = after(swap(rows), sibling_sources)
    arrived = exchange(pack_rows(rows, sibling_rows, share, swap(share)))
    picked = pick(sources, arrived)
    whole = []
    for own in picked:
        if whole:
            own = after(own, whole[0][-1])
        whole.append([own] + [turn(own, -shift) for shift in range(1, N_TP)])
    held = ()
    grads = []
    for group, (first, spans) in enumerate(GROUPS):
        *held, first_piece, second, third, fourth = attention(
            whole[group], kw, vw, queries[0], ctx_grad[0], first, spans, held
        )
        turned = [turn(x, by) for by, x in ((1, second), (2, third), (3, fourth))]
        grads.append(sum_parts([first_piece] + turned))
    context, query_grad = held
    passed = section_back(query_grad)
    messages = place(sources, sibling_sources, grads + [swap(grad) for grad in grads])
    returned = exchange(messages)
    encoded_grad = jnp.swapaxes(collect(rows, returned), 1, 2)
    passed = deliver([after(passed, returned[3])])
    return (context[None], passed[None], encoded_grad[None])


def solution(mesh):
    placed = (
        P("section", "seq", "tp"),
        P("section", "seq", None, None),
        P("section", "seq", None),
        P("section", "seq", None, None),
        P("section", None, "tp"),
        P("section", None, "tp"),
        P("section", "seq", "tp"),
    )
    return jax.shard_map(
        body,
        mesh=mesh,
        in_specs=placed,
        out_specs=(
            P("section", "seq", "tp"),
            P("section", "seq", "tp"),
            P("section", "seq", None, "tp"),
        ),
        check_vma=False,
    )
```

```python
import functools
import math

import jax
import jax.numpy as jnp
from jax import lax
from jax.experimental import pallas as pl
from jax.experimental.pallas import tpu as pltpu
from jax.sharding import PartitionSpec as P

DH = 128
E = 896
SPAN = 64
KNB = 2
NTOK = 128
N_SEQ = 16
CHIPS = N_SEQ // 2
CAP = 2
N_TP = 4
SLOTS = N_SEQ * CAP
REQ = 12
STORED = 16
SPANS_DEV = 6
TOKENS_DEV = SPANS_DEV * SPAN
HEADS_DEV = 8
WIDTH = HEADS_DEV * DH
PART = NTOK // N_TP
EQ = E // N_TP
KEYS = KNB * NTOK
GROUPS = ((0, 3), (3, 3))
HALVES = 2
ROWS = PART // HALVES
VMEM = 24 * 1024 * 1024
WIDE_VMEM = 60 * 1024 * 1024
BF16 = jnp.bfloat16
F32 = jnp.float32
SCALE = 1.0 / math.sqrt(DH)
IN_SMEM = pl.BlockSpec(memory_space=pltpu.SMEM)
IN_VMEM = pl.BlockSpec(memory_space=pltpu.VMEM)
ANYWHERE = pl.BlockSpec(memory_space=pl.ANY)


def params(limit=VMEM):
    return pltpu.CompilerParams(vmem_limit_bytes=limit)


def cost(flops, bytes_accessed):
    return pl.CostEstimate(flops=flops, bytes_accessed=bytes_accessed, transcendentals=0)


def dot(a, b):
    return jnp.dot(a, b, preferred_element_type=F32)


def dot_nt(a, b):
    return lax.dot_general(a, b, (((1,), (1,)), ((), ())), preferred_element_type=F32)


def dot_tn(a, b):
    return lax.dot_general(a, b, (((0,), (0,)), ((), ())), preferred_element_type=F32)


def member(shift):
    return lax.rem(lax.axis_index("tp") + shift, N_TP)


def share_kernel(encoded_ref, out_ref, sem):
    start = pl.multiple_of(lax.axis_index("tp") * PART, PART)
    copy = pltpu.make_async_copy(encoded_ref.at[:, pl.ds(start, PART)], out_ref, sem)
    copy.start()
    copy.wait()


def take_share(encoded):
    return pl.pallas_call(
        share_kernel,
        out_shape=jax.ShapeDtypeStruct((STORED, PART, E), BF16),
        in_specs=[ANYWHERE],
        out_specs=IN_VMEM,
        scratch_shapes=[pltpu.SemaphoreType.DMA],
        compiler_params=params(WIDE_VMEM),
        cost_estimate=cost(0, 2_000_000),
        name="take_share",
    )(encoded)


def pack_kernel(rows_ref, sibling_rows_ref, share_ref, sibling_ref, *outs):
    me = lax.axis_index("seq")
    chip, core = me // 2, lax.rem(me, 2)
    for ahead in range(CHIPS):
        device = lax.rem(chip + ahead, CHIPS) * 2 + core
        for j in range(CAP):
            row = jnp.clip(rows_ref[device, j], 0, STORED - 1)
            outs[ahead][j] = share_ref[row]
            row = jnp.clip(sibling_rows_ref[device, j], 0, STORED - 1)
            outs[ahead][CAP + j] = sibling_ref[row]


def pack_rows(rows, sibling_rows, share, sibling):
    return pl.pallas_call(
        pack_kernel,
        out_shape=[jax.ShapeDtypeStruct((2 * CAP, PART, E), BF16)] * CHIPS,
        in_specs=[IN_SMEM, IN_SMEM, IN_VMEM, IN_VMEM],
        out_specs=[IN_VMEM] * CHIPS,
        compiler_params=params(WIDE_VMEM),
        cost_estimate=cost(0, 3_000_000),
        name="pack_rows",
    )(rows, sibling_rows, share, sibling)


def places_of(neighbour_ref):
    me = lax.axis_index("seq")
    chip, core = me // 2, lax.rem(me, 2)
    sources = [neighbour_ref[r // KNB, r % KNB] for r in range(REQ)]
    places = []
    for r in range(REQ):
        earlier = jnp.int32(0)
        for q in range(r):
            earlier = earlier + (sources[q] == sources[r]).astype(jnp.int32)
        away = lax.rem(sources[r] // 2 - chip + CHIPS, CHIPS)
        other = (lax.rem(sources[r], 2) != core).astype(jnp.int32)
        places.append((away, other, jnp.minimum(earlier, CAP - 1)))
    return places


def pick_kernel(neighbour_ref, *refs):
    arrived, outs, table = refs[:CHIPS], refs[CHIPS:-1], refs[-1]
    for at in range(SLOTS):
        table[at] = REQ
    for r, (away, other, slot) in enumerate(places_of(neighbour_ref)):
        table[away * 2 * CAP + other * CAP + slot] = r
    half = GROUPS[0][1] * KNB
    for away in range(CHIPS):
        for block in range(2 * CAP):
            r = table[away * 2 * CAP + block]
            ref = arrived[(CHIPS - away) % CHIPS]

            @pl.when(r < half)
            def _():
                for n in range(HALVES):
                    outs[0][n, r] = ref[block, n * ROWS : (n + 1) * ROWS]

            @pl.when((r >= half) & (r < REQ))
            def _():
                for n in range(HALVES):
                    outs[1][n, r - half] = ref[block, n * ROWS : (n + 1) * ROWS]


def pick(neighbour, arrived):
    return pl.pallas_call(
        pick_kernel,
        out_shape=[
            jax.ShapeDtypeStruct((HALVES, spans * KNB, ROWS, E), BF16) for first, spans in GROUPS
        ],
        in_specs=[IN_SMEM] + [IN_VMEM] * CHIPS,
        out_specs=[IN_VMEM] * len(GROUPS),
        scratch_shapes=[pltpu.SMEM((SLOTS,), jnp.int32)],
        compiler_params=params(),
        cost_estimate=cost(0, 3_000_000),
        name="pick",
    )(neighbour, *arrived)


def attention_kernel(hops, *refs):
    pieces = refs[:hops]
    kw_ref, vw_ref, q_ref, g_ref = refs[hops : hops + 4]
    ctx_ref, qg_ref = refs[-(N_TP + 8) : -(N_TP + 6)]
    outs = refs[-(N_TP + 6) : -6]
    xs, ks, vs, kgs, vgs, backs = refs[-6:]
    step = pl.program_id(0)

    @pl.when(step == 0)
    def _():
        order = (0, 1, 2, 3) if hops == N_TP else (0, 1, 2, 2, 3)
        for n, shift in enumerate(order):
            ref = pieces[n]
            halves = [n - 2] if len(ref.shape) == 3 else range(HALVES)
            for half in halves:
                begin = pl.multiple_of(member(shift) * PART + half * ROWS, ROWS)
                for r in range(ref.shape[-3]):
                    piece = ref[r] if len(ref.shape) == 3 else ref[half, r]
                    xs[r, pl.ds(begin, ROWS), :] = piece
        x = xs[...].reshape(-1, E)
        ks[...] = dot(x, kw_ref[...]).astype(BF16)
        vs[...] = dot(x, vw_ref[...]).astype(BF16)

    mine = pl.ds(pl.multiple_of(step * KEYS, KEYS), KEYS)
    cols = [slice(h * DH, (h + 1) * DH) for h in range(HEADS_DEV)]
    scores = [dot_nt(q_ref[:, c], ks[mine, c]) for c in cols]
    prob_grads = [dot_nt(g_ref[:, c], vs[mine, c]) for c in cols]
    lows, dscores = [], []
    for score, prob_grad in zip(scores, prob_grads):
        exponent = jnp.exp(score * SCALE)
        probs = exponent / jnp.sum(exponent, axis=-1, keepdims=True)
        delta = jnp.sum(probs * prob_grad, axis=-1, keepdims=True)
        lows.append(probs.astype(BF16))
        dscores.append((probs * (prob_grad - delta) * SCALE).astype(BF16))
    for c, low, dscore in zip(cols, lows, dscores):
        kgs[c, :] = dot_tn(q_ref[:, c], dscore).astype(BF16)
        vgs[c, :] = dot_tn(g_ref[:, c], low).astype(BF16)
    for c, low, dscore in zip(cols, lows, dscores):
        ctx_ref[:, c] = dot(low, vs[mine, c]).astype(BF16)
        qg_ref[:, c] = dot(dscore, ks[mine, c]).astype(BF16)
    backs[...] = (dot(kw_ref[...], kgs[...]) + dot(vw_ref[...], vgs[...])).astype(BF16)
    for shift in range(N_TP):
        begin = pl.multiple_of(member(shift) * EQ, 16)
        for k in range(KNB):
            outs[shift][k] = backs[pl.ds(begin, EQ), k * NTOK : (k + 1) * NTOK]


def attention(pieces, kw, vw, queries, ctx_grad, first, spans, held):
    whole = pl.BlockSpec((E, WIDTH), lambda c: (0, 0))
    span = pl.BlockSpec((SPAN, WIDTH), lambda c: (c + first, 0))
    back = pl.BlockSpec((KNB, EQ, NTOK), lambda c: (c, 0, 0))
    wide = jax.ShapeDtypeStruct((TOKENS_DEV, WIDTH), BF16)
    piece = jax.ShapeDtypeStruct((spans * KNB, EQ, NTOK), BF16)
    hops = len(pieces)
    return pl.pallas_call(
        functools.partial(attention_kernel, hops),
        grid=(spans,),
        out_shape=[wide, wide] + [piece] * N_TP,
        in_specs=[IN_VMEM] * hops + [whole, whole, span, span] + [ANYWHERE] * len(held),
        out_specs=[span, span] + [back] * N_TP,
        scratch_shapes=[
            pltpu.VMEM((spans * KNB, NTOK, E), BF16),
            pltpu.VMEM((spans * KEYS, WIDTH), BF16),
            pltpu.VMEM((spans * KEYS, WIDTH), BF16),
            pltpu.VMEM((WIDTH, KEYS), BF16),
            pltpu.VMEM((WIDTH, KEYS), BF16),
            pltpu.VMEM((E, KEYS), BF16),
        ],
        input_output_aliases={hops + 4 + i: i for i in range(len(held))},
        compiler_params=params(),
        cost_estimate=cost(spans * 2_200_000_000, 5_000_000 + spans * 1_500_000),
        name="attention",
    )(*pieces, kw, vw, queries, ctx_grad, *held)


def sum_kernel(*refs):
    out_ref = refs[-1]
    for r in range(out_ref.shape[0]):
        total = refs[0][r].astype(F32)
        for part in refs[1:-1]:
            total = total + part[r].astype(F32)
        out_ref[r] = total.astype(BF16)


def sum_parts(parts):
    return pl.pallas_call(
        sum_kernel,
        out_shape=jax.ShapeDtypeStruct(parts[0].shape, BF16),
        in_specs=[IN_VMEM] * len(parts),
        out_specs=IN_VMEM,
        compiler_params=params(),
        cost_estimate=cost(0, 2_000_000),
        name="sum_parts",
    )(*parts)


def place_kernel(neighbour_ref, sibling_neighbour_ref, *refs):
    grads, outs, table = refs[:4], refs[4:-1], refs[-1]
    half = GROUPS[0][1] * KNB
    for at in range(SLOTS):
        table[at] = REQ
    for whose, ref in enumerate((neighbour_ref, sibling_neighbour_ref)):
        for r, (away, other, slot) in enumerate(places_of(ref)):
            at = away * 2 * CAP + whose * CAP + slot

            @pl.when(other == 0)
            def _():
                table[at] = r

    for away in range(CHIPS):
        for block in range(2 * CAP):
            r = table[away * 2 * CAP + block]
            low, high = grads[2 * (block // CAP)], grads[2 * (block // CAP) + 1]
            out = outs[away]

            @pl.when(r < half)
            def _():
                out[block] = low[r]

            @pl.when((r >= half) & (r < REQ))
            def _():
                out[block] = high[r - half]

            @pl.when(r >= REQ)
            def _():
                out[block] = jnp.zeros((EQ, NTOK), BF16)


def place(neighbour, sibling_neighbour, grads):
    return pl.pallas_call(
        place_kernel,
        out_shape=[jax.ShapeDtypeStruct((2 * CAP, EQ, NTOK), BF16)] * CHIPS,
        in_specs=[IN_SMEM, IN_SMEM] + [IN_VMEM] * len(grads),
        out_specs=[IN_VMEM] * CHIPS,
        scratch_shapes=[pltpu.SMEM((SLOTS,), jnp.int32)],
        compiler_params=params(),
        cost_estimate=cost(0, 3_000_000),
        name="place",
    )(neighbour, sibling_neighbour, *grads)


def collect_kernel(rows_ref, *refs):
    arrived, (out_ref, acc) = refs[:CHIPS], refs[CHIPS:]
    me = lax.axis_index("seq")
    chip, core = me // 2, lax.rem(me, 2)
    acc[...] = jnp.zeros(acc.shape, F32)
    for behind in range(CHIPS):
        device = lax.rem(chip - behind + CHIPS, CHIPS) * 2
        for block in range(2 * CAP):
            requester = device + (core if block < CAP else 1 - core)
            row = jnp.clip(rows_ref[requester, block % CAP], 0, STORED - 1)
            acc[row] += arrived[behind][block].astype(F32)
    out_ref[...] = acc[...].astype(BF16)


def collect(rows, arrived):
    return pl.pallas_call(
        collect_kernel,
        out_shape=jax.ShapeDtypeStruct((STORED, EQ, NTOK), BF16),
        in_specs=[IN_SMEM] + [IN_VMEM] * CHIPS,
        out_specs=IN_VMEM,
        scratch_shapes=[pltpu.VMEM((STORED, EQ, NTOK), F32)],
        compiler_params=params(),
        cost_estimate=cost(0, 3_000_000),
        name="collect",
    )(rows, *arrived)


def swap(x):
    return lax.ppermute(x, "seq", [(i, i ^ 1) for i in range(N_SEQ)])


def ahead(x, by):
    return lax.ppermute(x, "seq", [(i, (i + 2 * by) % N_SEQ) for i in range(N_SEQ)])


def after(x, *done):
    return lax.optimization_barrier((x,) + done)[0]


def exchange(messages):
    arrived = [messages[0]] + [None] * (CHIPS - 1)
    for by, behind in ((3, 0), (5, 0), (4, 0), (2, 0), (6, 0), (1, 3), (7, 5)):
        message = messages[by]
        if behind:
            message = after(message, arrived[behind])
        arrived[by] = ahead(message, by)
    return arrived


def turn(x, by):
    return lax.ppermute(x, "tp", [(i, (i + by) % N_TP) for i in range(N_TP)])


def section_back(x):
    count = lax.axis_size("section")
    return lax.ppermute(x, "section", [(i, i - 1) for i in range(1, count)])


def deliver_kernel(*refs):
    out_ref = refs[-1]
    at = 0
    for ref in refs[:-1]:
        rows = ref.shape[0]
        out_ref[at : at + rows] = ref[...]
        at += rows


def deliver(parts):
    return pl.pallas_call(
        deliver_kernel,
        out_shape=jax.ShapeDtypeStruct((TOKENS_DEV, WIDTH), BF16),
        in_specs=[IN_VMEM] * len(parts),
        out_specs=IN_VMEM,
        compiler_params=params(),
        cost_estimate=cost(0, 2_000_000),
        name="deliver",
    )(*parts)


def body(queries, encoded, neighbour, send_rows, key_weight, value_weight, ctx_grad):
    sources, rows = neighbour[0], send_rows[0, 0]
    kw, vw = key_weight[0], value_weight[0]
    share = take_share(encoded[0])
    sibling_sources = swap(sources)
    sibling_rows = after(swap(rows), sibling_sources)
    arrived = exchange(pack_rows(rows, sibling_rows, share, swap(share)))
    picked = pick(sources, arrived)
    low, high = turn(picked[0], 1), turn(picked[0], -1)
    across = [turn(low[0], 1), turn(high[1], -1)]
    whole = [[picked[0], high] + across + [low]]
    own = after(picked[1], low, high)
    whole.append([own] + [turn(own, -shift) for shift in range(1, N_TP)])
    held = ()
    grads = []
    for group, (first, spans) in enumerate(GROUPS):
        *held, first_piece, second, third, fourth = attention(
            whole[group], kw, vw, queries[0], ctx_grad[0], first, spans, held
        )
        turned = [turn(x, by) for by, x in ((1, second), (2, third), (3, fourth))]
        grads.append(sum_parts([first_piece] + turned))
    context, query_grad = held
    passed = section_back(query_grad)
    messages = place(sources, sibling_sources, grads + [swap(grad) for grad in grads])
    returned = exchange(messages)
    encoded_grad = jnp.swapaxes(collect(rows, returned), 1, 2)
    passed = deliver([after(passed, returned[3])])
    return (context[None], passed[None], encoded_grad[None])


def solution(mesh):
    placed = (
        P("section", "seq", "tp"),
        P("section", "seq", None, None),
        P("section", "seq", None),
        P("section", "seq", None, None),
        P("section", None, "tp"),
        P("section", None, "tp"),
        P("section", "seq", "tp"),
    )
    return jax.shard_map(
        body,
        mesh=mesh,
        in_specs=placed,
        out_specs=(
            P("section", "seq", "tp"),
            P("section", "seq", "tp"),
            P("section", "seq", None, "tp"),
        ),
        check_vma=False,
    )
```

```python
import functools
import math

import jax
import jax.numpy as jnp
from jax import lax
from jax.experimental import pallas as pl
from jax.experimental.pallas import tpu as pltpu
from jax.sharding import PartitionSpec as P

DH = 128
E = 896
SPAN = 64
KNB = 2
NTOK = 128
N_SEQ = 16
CHIPS = N_SEQ // 2
CAP = 2
N_TP = 4
SLOTS = N_SEQ * CAP
REQ = 12
STORED = 16
SPANS_DEV = 6
TOKENS_DEV = SPANS_DEV * SPAN
HEADS_DEV = 8
WIDTH = HEADS_DEV * DH
PART = NTOK // N_TP
EQ = E // N_TP
KEYS = KNB * NTOK
GROUPS = ((0, 3), (3, 3))
HALVES = 2
ROWS = PART // HALVES
VMEM = 24 * 1024 * 1024
WIDE_VMEM = 60 * 1024 * 1024
BF16 = jnp.bfloat16
F32 = jnp.float32
SCALE = 1.0 / math.sqrt(DH)
IN_SMEM = pl.BlockSpec(memory_space=pltpu.SMEM)
IN_VMEM = pl.BlockSpec(memory_space=pltpu.VMEM)
ANYWHERE = pl.BlockSpec(memory_space=pl.ANY)


def params(limit=VMEM):
    return pltpu.CompilerParams(vmem_limit_bytes=limit)


def cost(flops, bytes_accessed):
    return pl.CostEstimate(flops=flops, bytes_accessed=bytes_accessed, transcendentals=0)


def dot(a, b):
    return jnp.dot(a, b, preferred_element_type=F32)


def dot_nt(a, b):
    return lax.dot_general(a, b, (((1,), (1,)), ((), ())), preferred_element_type=F32)


def dot_tn(a, b):
    return lax.dot_general(a, b, (((0,), (0,)), ((), ())), preferred_element_type=F32)


def member(shift):
    return lax.rem(lax.axis_index("tp") + shift, N_TP)


def share_kernel(encoded_ref, out_ref, sem):
    start = pl.multiple_of(lax.axis_index("tp") * PART, PART)
    copy = pltpu.make_async_copy(encoded_ref.at[:, pl.ds(start, PART)], out_ref, sem)
    copy.start()
    copy.wait()


def take_share(encoded):
    return pl.pallas_call(
        share_kernel,
        out_shape=jax.ShapeDtypeStruct((STORED, PART, E), BF16),
        in_specs=[ANYWHERE],
        out_specs=IN_VMEM,
        scratch_shapes=[pltpu.SemaphoreType.DMA],
        compiler_params=params(WIDE_VMEM),
        cost_estimate=cost(0, 2_000_000),
        name="take_share",
    )(encoded)


def pack_kernel(rows_ref, sibling_rows_ref, share_ref, sibling_ref, *outs):
    me = lax.axis_index("seq")
    chip, core = me // 2, lax.rem(me, 2)
    for ahead in range(CHIPS):
        device = lax.rem(chip + ahead, CHIPS) * 2 + core
        for j in range(CAP):
            row = jnp.clip(rows_ref[device, j], 0, STORED - 1)
            outs[ahead][j] = share_ref[row]
            row = jnp.clip(sibling_rows_ref[device, j], 0, STORED - 1)
            outs[ahead][CAP + j] = sibling_ref[row]


def pack_rows(rows, sibling_rows, share, sibling):
    return pl.pallas_call(
        pack_kernel,
        out_shape=[jax.ShapeDtypeStruct((2 * CAP, PART, E), BF16)] * CHIPS,
        in_specs=[IN_SMEM, IN_SMEM, IN_VMEM, IN_VMEM],
        out_specs=[IN_VMEM] * CHIPS,
        compiler_params=params(WIDE_VMEM),
        cost_estimate=cost(0, 3_000_000),
        name="pack_rows",
    )(rows, sibling_rows, share, sibling)


def places_of(neighbour_ref):
    me = lax.axis_index("seq")
    chip, core = me // 2, lax.rem(me, 2)
    sources = [neighbour_ref[r // KNB, r % KNB] for r in range(REQ)]
    places = []
    for r in range(REQ):
        earlier = jnp.int32(0)
        for q in range(r):
            earlier = earlier + (sources[q] == sources[r]).astype(jnp.int32)
        away = lax.rem(sources[r] // 2 - chip + CHIPS, CHIPS)
        other = (lax.rem(sources[r], 2) != core).astype(jnp.int32)
        places.append((away, other, jnp.minimum(earlier, CAP - 1)))
    return places


def pick_kernel(neighbour_ref, *refs):
    arrived, outs, table = refs[:CHIPS], refs[CHIPS:-1], refs[-1]
    for at in range(SLOTS):
        table[at] = REQ
    for r, (away, other, slot) in enumerate(places_of(neighbour_ref)):
        table[away * 2 * CAP + other * CAP + slot] = r
    half = GROUPS[0][1] * KNB
    for away in range(CHIPS):
        for block in range(2 * CAP):
            r = table[away * 2 * CAP + block]
            ref = arrived[(CHIPS - away) % CHIPS]

            @pl.when(r < half)
            def _():
                for n in range(HALVES):
                    outs[0][n, r] = ref[block, n * ROWS : (n + 1) * ROWS]

            @pl.when((r >= half) & (r < REQ))
            def _():
                for n in range(HALVES):
                    outs[1][n, r - half] = ref[block, n * ROWS : (n + 1) * ROWS]


def pick(neighbour, arrived):
    return pl.pallas_call(
        pick_kernel,
        out_shape=[
            jax.ShapeDtypeStruct((HALVES, spans * KNB, ROWS, E), BF16) for first, spans in GROUPS
        ],
        in_specs=[IN_SMEM] + [IN_VMEM] * CHIPS,
        out_specs=[IN_VMEM] * len(GROUPS),
        scratch_shapes=[pltpu.SMEM((SLOTS,), jnp.int32)],
        compiler_params=params(),
        cost_estimate=cost(0, 3_000_000),
        name="pick",
    )(neighbour, *arrived)


def project_kernel(count, *refs):
    pieces, (kw_ref, vw_ref) = refs[:count], refs[count : count + 2]
    outs = refs[count + 2 :]
    for n, piece in enumerate(pieces):
        x = piece[...].reshape(-1, E)
        for w_ref, out in ((kw_ref, outs[2 * n]), (vw_ref, outs[2 * n + 1])):
            out[...] = dot(x, w_ref[...]).astype(BF16).reshape(out.shape)


def project(pieces, kw, vw):
    outs = [jax.ShapeDtypeStruct(piece.shape[:-1] + (WIDTH,), BF16) for piece in pieces]
    results = pl.pallas_call(
        functools.partial(project_kernel, len(pieces)),
        out_shape=[out for out in outs for _ in range(2)],
        in_specs=[IN_VMEM] * (len(pieces) + 2),
        out_specs=[IN_VMEM] * (2 * len(pieces)),
        compiler_params=params(),
        cost_estimate=cost(1_500_000_000, 6_000_000),
        name="project",
    )(*pieces, kw, vw)
    return [results[2 * n : 2 * n + 2] for n in range(len(pieces))]


def attention_kernel(known, raw, *refs):
    ready, arrived = refs[: 2 * len(known)], refs[2 * len(known) : 2 * len(known) + len(raw)]
    at = 2 * len(known) + len(raw)
    kw_ref, vw_ref, q_ref, g_ref = refs[at : at + 4]
    ctx_ref, qg_ref = refs[-(N_TP + 8) : -(N_TP + 6)]
    outs = refs[-(N_TP + 6) : -6]
    xs, ks, vs, kgs, vgs, backs = refs[-6:]
    step = pl.program_id(0)

    @pl.when(step == 0)
    def _():
        def rows_of(shift, half, r):
            begin = r * NTOK + member(shift) * PART + half * ROWS
            return pl.ds(pl.multiple_of(begin, ROWS), ROWS)

        requests = ks.shape[0] // NTOK
        for n, shift in enumerate(known):
            for half in range(HALVES):
                for r in range(requests):
                    ks[rows_of(shift, half, r), :] = ready[2 * n][half, r]
                    vs[rows_of(shift, half, r), :] = ready[2 * n + 1][half, r]
        spots = []
        for ref, (shift, halves) in zip(arrived, raw):
            for half in halves:
                for r in range(requests):
                    piece = ref[r] if len(halves) == 1 else ref[half, r]
                    xs[len(spots) * ROWS : (len(spots) + 1) * ROWS, :] = piece
                    spots.append(rows_of(shift, half, r))
        for w_ref, out in ((kw_ref, ks), (vw_ref, vs)):
            found = dot(xs[...], w_ref[...]).astype(BF16)
            for n, spot in enumerate(spots):
                out[spot, :] = found[n * ROWS : (n + 1) * ROWS]

    mine = pl.ds(pl.multiple_of(step * KEYS, KEYS), KEYS)
    cols = [slice(h * DH, (h + 1) * DH) for h in range(HEADS_DEV)]
    scores = [dot_nt(q_ref[:, c], ks[mine, c]) for c in cols]
    prob_grads = [dot_nt(g_ref[:, c], vs[mine, c]) for c in cols]
    lows, dscores = [], []
    for score, prob_grad in zip(scores, prob_grads):
        exponent = jnp.exp(score * SCALE)
        probs = exponent / jnp.sum(exponent, axis=-1, keepdims=True)
        delta = jnp.sum(probs * prob_grad, axis=-1, keepdims=True)
        lows.append(probs.astype(BF16))
        dscores.append((probs * (prob_grad - delta) * SCALE).astype(BF16))
    for c, low, dscore in zip(cols, lows, dscores):
        kgs[c, :] = dot_tn(q_ref[:, c], dscore).astype(BF16)
        vgs[c, :] = dot_tn(g_ref[:, c], low).astype(BF16)
    for c, low, dscore in zip(cols, lows, dscores):
        ctx_ref[:, c] = dot(low, vs[mine, c]).astype(BF16)
        qg_ref[:, c] = dot(dscore, ks[mine, c]).astype(BF16)
    backs[...] = (dot(kw_ref[...], kgs[...]) + dot(vw_ref[...], vgs[...])).astype(BF16)
    for shift in range(N_TP):
        begin = pl.multiple_of(member(shift) * EQ, 16)
        for k in range(KNB):
            outs[shift][k] = backs[pl.ds(begin, EQ), k * NTOK : (k + 1) * NTOK]


def attention(known, raw, kw, vw, queries, ctx_grad, first, spans, held):
    whole = pl.BlockSpec((E, WIDTH), lambda c: (0, 0))
    span = pl.BlockSpec((SPAN, WIDTH), lambda c: (c + first, 0))
    back = pl.BlockSpec((KNB, EQ, NTOK), lambda c: (c, 0, 0))
    wide = jax.ShapeDtypeStruct((TOKENS_DEV, WIDTH), BF16)
    piece = jax.ShapeDtypeStruct((spans * KNB, EQ, NTOK), BF16)
    ready = [x for shift, pair in known for x in pair]
    arrived = [x for shift, halves, x in raw]
    at = len(ready) + len(arrived)
    raw_rows = sum(len(halves) for shift, halves, x in raw) * spans * KNB * ROWS
    return pl.pallas_call(
        functools.partial(
            attention_kernel,
            [shift for shift, pair in known],
            [(shift, halves) for shift, halves, x in raw],
        ),
        grid=(spans,),
        out_shape=[wide, wide] + [piece] * N_TP,
        in_specs=[IN_VMEM] * at + [whole, whole, span, span] + [ANYWHERE] * len(held),
        out_specs=[span, span] + [back] * N_TP,
        scratch_shapes=[
            pltpu.VMEM((raw_rows, E), BF16),
            pltpu.VMEM((spans * KEYS, WIDTH), BF16),
            pltpu.VMEM((spans * KEYS, WIDTH), BF16),
            pltpu.VMEM((WIDTH, KEYS), BF16),
            pltpu.VMEM((WIDTH, KEYS), BF16),
            pltpu.VMEM((E, KEYS), BF16),
        ],
        input_output_aliases={at + 4 + i: i for i in range(len(held))},
        compiler_params=params(),
        cost_estimate=cost(spans * 2_200_000_000, 5_000_000 + spans * 1_500_000),
        name="attention",
    )(*ready, *arrived, kw, vw, queries, ctx_grad, *held)


def sum_kernel(*refs):
    out_ref = refs[-1]
    for r in range(out_ref.shape[0]):
        total = refs[0][r].astype(F32)
        for part in refs[1:-1]:
            total = total + part[r].astype(F32)
        out_ref[r] = total.astype(BF16)


def sum_parts(parts):
    return pl.pallas_call(
        sum_kernel,
        out_shape=jax.ShapeDtypeStruct(parts[0].shape, BF16),
        in_specs=[IN_VMEM] * len(parts),
        out_specs=IN_VMEM,
        compiler_params=params(),
        cost_estimate=cost(0, 2_000_000),
        name="sum_parts",
    )(*parts)


def place_kernel(neighbour_ref, sibling_neighbour_ref, *refs):
    grads, outs, table = refs[:4], refs[4:-1], refs[-1]
    half = GROUPS[0][1] * KNB
    for at in range(SLOTS):
        table[at] = REQ
    for whose, ref in enumerate((neighbour_ref, sibling_neighbour_ref)):
        for r, (away, other, slot) in enumerate(places_of(ref)):
            at = away * 2 * CAP + whose * CAP + slot

            @pl.when(other == 0)
            def _():
                table[at] = r

    for away in range(CHIPS):
        for block in range(2 * CAP):
            r = table[away * 2 * CAP + block]
            low, high = grads[2 * (block // CAP)], grads[2 * (block // CAP) + 1]
            out = outs[away]

            @pl.when(r < half)
            def _():
                out[block] = low[r]

            @pl.when((r >= half) & (r < REQ))
            def _():
                out[block] = high[r - half]

            @pl.when(r >= REQ)
            def _():
                out[block] = jnp.zeros((EQ, NTOK), BF16)


def place(neighbour, sibling_neighbour, grads):
    return pl.pallas_call(
        place_kernel,
        out_shape=[jax.ShapeDtypeStruct((2 * CAP, EQ, NTOK), BF16)] * CHIPS,
        in_specs=[IN_SMEM, IN_SMEM] + [IN_VMEM] * len(grads),
        out_specs=[IN_VMEM] * CHIPS,
        scratch_shapes=[pltpu.SMEM((SLOTS,), jnp.int32)],
        compiler_params=params(),
        cost_estimate=cost(0, 3_000_000),
        name="place",
    )(neighbour, sibling_neighbour, *grads)


def collect_kernel(rows_ref, *refs):
    arrived, (out_ref, acc) = refs[:CHIPS], refs[CHIPS:]
    me = lax.axis_index("seq")
    chip, core = me // 2, lax.rem(me, 2)
    acc[...] = jnp.zeros(acc.shape, F32)
    for behind in range(CHIPS):
        device = lax.rem(chip - behind + CHIPS, CHIPS) * 2
        for block in range(2 * CAP):
            requester = device + (core if block < CAP else 1 - core)
            row = jnp.clip(rows_ref[requester, block % CAP], 0, STORED - 1)
            acc[row] += arrived[behind][block].astype(F32)
    out_ref[...] = acc[...].astype(BF16)


def collect(rows, arrived):
    return pl.pallas_call(
        collect_kernel,
        out_shape=jax.ShapeDtypeStruct((STORED, EQ, NTOK), BF16),
        in_specs=[IN_SMEM] + [IN_VMEM] * CHIPS,
        out_specs=IN_VMEM,
        scratch_shapes=[pltpu.VMEM((STORED, EQ, NTOK), F32)],
        compiler_params=params(),
        cost_estimate=cost(0, 3_000_000),
        name="collect",
    )(rows, *arrived)


def swap(x):
    return lax.ppermute(x, "seq", [(i, i ^ 1) for i in range(N_SEQ)])


def ahead(x, by):
    return lax.ppermute(x, "seq", [(i, (i + 2 * by) % N_SEQ) for i in range(N_SEQ)])


def after(x, *done):
    return lax.optimization_barrier((x,) + done)[0]


def exchange(messages):
    arrived = [messages[0]] + [None] * (CHIPS - 1)
    for by, behind in ((3, 0), (5, 0), (4, 0), (2, 0), (6, 0), (1, 3), (7, 5)):
        message = messages[by]
        if behind:
            message = after(message, arrived[behind])
        arrived[by] = ahead(message, by)
    return arrived


def turn(x, by):
    return lax.ppermute(x, "tp", [(i, (i + by) % N_TP) for i in range(N_TP)])


def section_back(x):
    count = lax.axis_size("section")
    return lax.ppermute(x, "section", [(i, i - 1) for i in range(1, count)])


def deliver_kernel(*refs):
    out_ref = refs[-1]
    at = 0
    for ref in refs[:-1]:
        rows = ref.shape[0]
        out_ref[at : at + rows] = ref[...]
        at += rows


def deliver(parts):
    return pl.pallas_call(
        deliver_kernel,
        out_shape=jax.ShapeDtypeStruct((TOKENS_DEV, WIDTH), BF16),
        in_specs=[IN_VMEM] * len(parts),
        out_specs=IN_VMEM,
        compiler_params=params(),
        cost_estimate=cost(0, 2_000_000),
        name="deliver",
    )(*parts)


def body(queries, encoded, neighbour, send_rows, key_weight, value_weight, ctx_grad):
    sources, rows = neighbour[0], send_rows[0, 0]
    kw, vw = key_weight[0], value_weight[0]
    share = take_share(encoded[0])
    sibling_sources = swap(sources)
    sibling_rows = after(swap(rows), sibling_sources)
    arrived = exchange(pack_rows(rows, sibling_rows, share, swap(share)))
    picked = pick(sources, arrived)
    low, high = turn(picked[0], 1), turn(picked[0], -1)
    own_first, own_second = project(picked, kw, vw)
    across = [turn(after(low, *own_first)[0], 1), turn(after(high, *own_first)[1], -1)]
    own = after(picked[1], low, high)
    others = [turn(own, -shift) for shift in range(1, N_TP)]
    next_first, last_first = project([high, low], kw, vw)
    both = tuple(range(HALVES))
    known = [
        [(0, own_first), (1, next_first), (3, last_first)],
        [(0, own_second)],
    ]
    raw = [
        [(2, (half,), x) for half, x in enumerate(across)],
        [(shift, both, x) for shift, x in enumerate(others, 1)],
    ]
    held = ()
    grads = []
    for group, (first, spans) in enumerate(GROUPS):
        *held, first_piece, second, third, fourth = attention(
            known[group], raw[group], kw, vw, queries[0], ctx_grad[0], first, spans, held
        )
        turned = [turn(x, by) for by, x in ((1, second), (2, third), (3, fourth))]
        grads.append(sum_parts([first_piece] + turned))
    context, query_grad = held
    passed = section_back(query_grad)
    messages = place(sources, sibling_sources, grads + [swap(grad) for grad in grads])
    returned = exchange(messages)
    encoded_grad = jnp.swapaxes(collect(rows, returned), 1, 2)
    passed = deliver([after(passed, returned[3])])
    return (context[None], passed[None], encoded_grad[None])


def solution(mesh):
    placed = (
        P("section", "seq", "tp"),
        P("section", "seq", None, None),
        P("section", "seq", None),
        P("section", "seq", None, None),
        P("section", None, "tp"),
        P("section", None, "tp"),
        P("section", "seq", "tp"),
    )
    return jax.shard_map(
        body,
        mesh=mesh,
        in_specs=placed,
        out_specs=(
            P("section", "seq", "tp"),
            P("section", "seq", "tp"),
            P("section", "seq", None, "tp"),
        ),
        check_vma=False,
    )
```

```python
import functools
import math

import jax
import jax.numpy as jnp
from jax import lax
from jax.experimental import pallas as pl
from jax.experimental.pallas import tpu as pltpu
from jax.sharding import PartitionSpec as P

DH = 128
E = 896
SPAN = 64
KNB = 2
NTOK = 128
N_SEQ = 16
CHIPS = N_SEQ // 2
CAP = 2
N_TP = 4
SLOTS = N_SEQ * CAP
REQ = 12
STORED = 16
SPANS_DEV = 6
TOKENS_DEV = SPANS_DEV * SPAN
HEADS_DEV = 8
WIDTH = HEADS_DEV * DH
PART = NTOK // N_TP
EQ = E // N_TP
KEYS = KNB * NTOK
GROUPS = ((0, 3), (3, 3))
HALVES = 2
ROWS = PART // HALVES
VMEM = 24 * 1024 * 1024
WIDE_VMEM = 60 * 1024 * 1024
BF16 = jnp.bfloat16
F32 = jnp.float32
SCALE = 1.0 / math.sqrt(DH)
IN_SMEM = pl.BlockSpec(memory_space=pltpu.SMEM)
IN_VMEM = pl.BlockSpec(memory_space=pltpu.VMEM)
ANYWHERE = pl.BlockSpec(memory_space=pl.ANY)


def params(limit=VMEM):
    return pltpu.CompilerParams(vmem_limit_bytes=limit)


def cost(flops, bytes_accessed):
    return pl.CostEstimate(flops=flops, bytes_accessed=bytes_accessed, transcendentals=0)


def dot(a, b):
    return jnp.dot(a, b, preferred_element_type=F32)


def dot_nt(a, b):
    return lax.dot_general(a, b, (((1,), (1,)), ((), ())), preferred_element_type=F32)


def dot_tn(a, b):
    return lax.dot_general(a, b, (((0,), (0,)), ((), ())), preferred_element_type=F32)


def member(shift):
    return lax.rem(lax.axis_index("tp") + shift, N_TP)


def share_kernel(encoded_ref, out_ref, sem):
    start = pl.multiple_of(lax.axis_index("tp") * PART, PART)
    copy = pltpu.make_async_copy(encoded_ref.at[:, pl.ds(start, PART)], out_ref, sem)
    copy.start()
    copy.wait()


def take_share(encoded):
    return pl.pallas_call(
        share_kernel,
        out_shape=jax.ShapeDtypeStruct((STORED, PART, E), BF16),
        in_specs=[ANYWHERE],
        out_specs=IN_VMEM,
        scratch_shapes=[pltpu.SemaphoreType.DMA],
        compiler_params=params(WIDE_VMEM),
        cost_estimate=cost(0, 2_000_000),
        name="take_share",
    )(encoded)


def pack_kernel(rows_ref, sibling_rows_ref, share_ref, sibling_ref, *outs):
    me = lax.axis_index("seq")
    chip, core = me // 2, lax.rem(me, 2)
    for ahead in range(CHIPS):
        device = lax.rem(chip + ahead, CHIPS) * 2 + core
        for j in range(CAP):
            row = jnp.clip(rows_ref[device, j], 0, STORED - 1)
            outs[ahead][j] = share_ref[row]
            row = jnp.clip(sibling_rows_ref[device, j], 0, STORED - 1)
            outs[ahead][CAP + j] = sibling_ref[row]


def pack_rows(rows, sibling_rows, share, sibling):
    return pl.pallas_call(
        pack_kernel,
        out_shape=[jax.ShapeDtypeStruct((2 * CAP, PART, E), BF16)] * CHIPS,
        in_specs=[IN_SMEM, IN_SMEM, IN_VMEM, IN_VMEM],
        out_specs=[IN_VMEM] * CHIPS,
        compiler_params=params(WIDE_VMEM),
        cost_estimate=cost(0, 3_000_000),
        name="pack_rows",
    )(rows, sibling_rows, share, sibling)


def places_of(neighbour_ref):
    me = lax.axis_index("seq")
    chip, core = me // 2, lax.rem(me, 2)
    sources = [neighbour_ref[r // KNB, r % KNB] for r in range(REQ)]
    places = []
    for r in range(REQ):
        earlier = jnp.int32(0)
        for q in range(r):
            earlier = earlier + (sources[q] == sources[r]).astype(jnp.int32)
        away = lax.rem(sources[r] // 2 - chip + CHIPS, CHIPS)
        other = (lax.rem(sources[r], 2) != core).astype(jnp.int32)
        places.append((away, other, jnp.minimum(earlier, CAP - 1)))
    return places


def pick_kernel(neighbour_ref, *refs):
    arrived, outs, table = refs[:CHIPS], refs[CHIPS:-1], refs[-1]
    for at in range(SLOTS):
        table[at] = REQ
    for r, (away, other, slot) in enumerate(places_of(neighbour_ref)):
        table[away * 2 * CAP + other * CAP + slot] = r
    half = GROUPS[0][1] * KNB
    for away in range(CHIPS):
        for block in range(2 * CAP):
            r = table[away * 2 * CAP + block]
            ref = arrived[(CHIPS - away) % CHIPS]

            @pl.when(r < half)
            def _():
                for n in range(HALVES):
                    outs[0][n, r] = ref[block, n * ROWS : (n + 1) * ROWS]

            @pl.when((r >= half) & (r < REQ))
            def _():
                for n in range(HALVES):
                    outs[1][n, r - half] = ref[block, n * ROWS : (n + 1) * ROWS]


def pick(neighbour, arrived):
    return pl.pallas_call(
        pick_kernel,
        out_shape=[
            jax.ShapeDtypeStruct((HALVES, spans * KNB, ROWS, E), BF16) for first, spans in GROUPS
        ],
        in_specs=[IN_SMEM] + [IN_VMEM] * CHIPS,
        out_specs=[IN_VMEM] * len(GROUPS),
        scratch_shapes=[pltpu.SMEM((SLOTS,), jnp.int32)],
        compiler_params=params(),
        cost_estimate=cost(0, 3_000_000),
        name="pick",
    )(neighbour, *arrived)


def project_kernel(count, *refs):
    pieces, (kw_ref, vw_ref) = refs[:count], refs[count : count + 2]
    outs = refs[count + 2 :]
    for n, piece in enumerate(pieces):
        x = piece[...].reshape(-1, E)
        for w_ref, out in ((kw_ref, outs[2 * n]), (vw_ref, outs[2 * n + 1])):
            out[...] = dot(x, w_ref[...]).astype(BF16).reshape(out.shape)


def project(pieces, kw, vw):
    outs = [jax.ShapeDtypeStruct(piece.shape[:-1] + (WIDTH,), BF16) for piece in pieces]
    results = pl.pallas_call(
        functools.partial(project_kernel, len(pieces)),
        out_shape=[out for out in outs for _ in range(2)],
        in_specs=[IN_VMEM] * (len(pieces) + 2),
        out_specs=[IN_VMEM] * (2 * len(pieces)),
        compiler_params=params(),
        cost_estimate=cost(1_500_000_000, 6_000_000),
        name="project",
    )(*pieces, kw, vw)
    return [results[2 * n : 2 * n + 2] for n in range(len(pieces))]


def attention_kernel(known, raw, *refs):
    ready, arrived = refs[: 2 * len(known)], refs[2 * len(known) : 2 * len(known) + len(raw)]
    at = 2 * len(known) + len(raw)
    kw_ref, vw_ref, q_ref, g_ref = refs[at : at + 4]
    ctx_ref, qg_ref = refs[-(N_TP + 8) : -(N_TP + 6)]
    outs = refs[-(N_TP + 6) : -6]
    xs, ks, vs, kgs, vgs, backs = refs[-6:]
    step = pl.program_id(0)

    @pl.when(step == 0)
    def _():
        def rows_of(shift, half, r):
            begin = r * NTOK + member(shift) * PART + half * ROWS
            return pl.ds(pl.multiple_of(begin, ROWS), ROWS)

        requests = ks.shape[0] // NTOK
        for n, shift in enumerate(known):
            for half in range(HALVES):
                for r in range(requests):
                    ks[rows_of(shift, half, r), :] = ready[2 * n][half, r]
                    vs[rows_of(shift, half, r), :] = ready[2 * n + 1][half, r]
        spots = []
        for ref, (shift, halves) in zip(arrived, raw):
            for half in halves:
                for r in range(requests):
                    piece = ref[r] if len(halves) == 1 else ref[half, r]
                    xs[len(spots) * ROWS : (len(spots) + 1) * ROWS, :] = piece
                    spots.append(rows_of(shift, half, r))
        for w_ref, out in ((kw_ref, ks), (vw_ref, vs)):
            found = dot(xs[...], w_ref[...]).astype(BF16)
            for n, spot in enumerate(spots):
                out[spot, :] = found[n * ROWS : (n + 1) * ROWS]

    mine = pl.ds(pl.multiple_of(step * KEYS, KEYS), KEYS)
    cols = [slice(h * DH, (h + 1) * DH) for h in range(HEADS_DEV)]
    scores = [dot_nt(q_ref[:, c], ks[mine, c]) for c in cols]
    prob_grads = [dot_nt(g_ref[:, c], vs[mine, c]) for c in cols]
    lows, dscores = [], []
    for score, prob_grad in zip(scores, prob_grads):
        exponent = jnp.exp(score * SCALE)
        probs = exponent / jnp.sum(exponent, axis=-1, keepdims=True)
        delta = jnp.sum(probs * prob_grad, axis=-1, keepdims=True)
        lows.append(probs.astype(BF16))
        dscores.append((probs * (prob_grad - delta) * SCALE).astype(BF16))
    for c, low, dscore in zip(cols, lows, dscores):
        kgs[c, :] = dot_tn(q_ref[:, c], dscore).astype(BF16)
        vgs[c, :] = dot_tn(g_ref[:, c], low).astype(BF16)
    for c, low, dscore in zip(cols, lows, dscores):
        ctx_ref[:, c] = dot(low, vs[mine, c]).astype(BF16)
        qg_ref[:, c] = dot(dscore, ks[mine, c]).astype(BF16)
    backs[...] = (dot(kw_ref[...], kgs[...]) + dot(vw_ref[...], vgs[...])).astype(BF16)
    for shift in range(N_TP):
        begin = pl.multiple_of(member(shift) * EQ, 16)
        for k in range(KNB):
            outs[shift][k] = backs[pl.ds(begin, EQ), k * NTOK : (k + 1) * NTOK]


def attention(known, raw, kw, vw, queries, ctx_grad, first, spans, held):
    whole = pl.BlockSpec((E, WIDTH), lambda c: (0, 0))
    span = pl.BlockSpec((SPAN, WIDTH), lambda c: (c + first, 0))
    back = pl.BlockSpec((KNB, EQ, NTOK), lambda c: (c, 0, 0))
    wide = jax.ShapeDtypeStruct((TOKENS_DEV, WIDTH), BF16)
    piece = jax.ShapeDtypeStruct((spans * KNB, EQ, NTOK), BF16)
    ready = [x for shift, pair in known for x in pair]
    arrived = [x for shift, halves, x in raw]
    at = len(ready) + len(arrived)
    raw_rows = sum(len(halves) for shift, halves, x in raw) * spans * KNB * ROWS
    return pl.pallas_call(
        functools.partial(
            attention_kernel,
            [shift for shift, pair in known],
            [(shift, halves) for shift, halves, x in raw],
        ),
        grid=(spans,),
        out_shape=[wide, wide] + [piece] * N_TP,
        in_specs=[IN_VMEM] * at + [whole, whole, span, span] + [ANYWHERE] * len(held),
        out_specs=[span, span] + [back] * N_TP,
        scratch_shapes=[
            pltpu.VMEM((raw_rows, E), BF16),
            pltpu.VMEM((spans * KEYS, WIDTH), BF16),
            pltpu.VMEM((spans * KEYS, WIDTH), BF16),
            pltpu.VMEM((WIDTH, KEYS), BF16),
            pltpu.VMEM((WIDTH, KEYS), BF16),
            pltpu.VMEM((E, KEYS), BF16),
        ],
        input_output_aliases={at + 4 + i: i for i in range(len(held))},
        compiler_params=params(),
        cost_estimate=cost(spans * 2_200_000_000, 5_000_000 + spans * 1_500_000),
        name="attention",
    )(*ready, *arrived, kw, vw, queries, ctx_grad, *held)


def sum_kernel(*refs):
    out_ref = refs[-1]
    for r in range(out_ref.shape[0]):
        total = refs[0][r].astype(F32)
        for part in refs[1:-1]:
            total = total + part[r].astype(F32)
        out_ref[r] = total.astype(BF16)


def sum_parts(parts):
    return pl.pallas_call(
        sum_kernel,
        out_shape=jax.ShapeDtypeStruct(parts[0].shape, BF16),
        in_specs=[IN_VMEM] * len(parts),
        out_specs=IN_VMEM,
        compiler_params=params(),
        cost_estimate=cost(0, 2_000_000),
        name="sum_parts",
    )(*parts)


def place_kernel(neighbour_ref, sibling_neighbour_ref, *refs):
    grads, outs, table = refs[:4], refs[4:-1], refs[-1]
    half = GROUPS[0][1] * KNB
    for at in range(SLOTS):
        table[at] = REQ
    for whose, ref in enumerate((neighbour_ref, sibling_neighbour_ref)):
        for r, (away, other, slot) in enumerate(places_of(ref)):
            at = away * 2 * CAP + whose * CAP + slot

            @pl.when(other == 0)
            def _():
                table[at] = r

    for away in range(CHIPS):
        for block in range(2 * CAP):
            r = table[away * 2 * CAP + block]
            low, high = grads[2 * (block // CAP)], grads[2 * (block // CAP) + 1]
            out = outs[away]

            @pl.when(r < half)
            def _():
                out[block] = low[r]

            @pl.when((r >= half) & (r < REQ))
            def _():
                out[block] = high[r - half]

            @pl.when(r >= REQ)
            def _():
                out[block] = jnp.zeros((EQ, NTOK), BF16)


def place(neighbour, sibling_neighbour, grads):
    return pl.pallas_call(
        place_kernel,
        out_shape=[jax.ShapeDtypeStruct((2 * CAP, EQ, NTOK), BF16)] * CHIPS,
        in_specs=[IN_SMEM, IN_SMEM] + [IN_VMEM] * len(grads),
        out_specs=[IN_VMEM] * CHIPS,
        scratch_shapes=[pltpu.SMEM((SLOTS,), jnp.int32)],
        compiler_params=params(),
        cost_estimate=cost(0, 3_000_000),
        name="place",
    )(neighbour, sibling_neighbour, *grads)


def collect_kernel(rows_ref, *refs):
    arrived, (out_ref, acc) = refs[:CHIPS], refs[CHIPS:]
    me = lax.axis_index("seq")
    chip, core = me // 2, lax.rem(me, 2)
    acc[...] = jnp.zeros(acc.shape, F32)
    for behind in range(CHIPS):
        device = lax.rem(chip - behind + CHIPS, CHIPS) * 2
        for block in range(2 * CAP):
            requester = device + (core if block < CAP else 1 - core)
            row = jnp.clip(rows_ref[requester, block % CAP], 0, STORED - 1)
            acc[row] += arrived[behind][block].astype(F32)
    out_ref[...] = acc[...].astype(BF16)


def collect(rows, arrived):
    return pl.pallas_call(
        collect_kernel,
        out_shape=jax.ShapeDtypeStruct((STORED, EQ, NTOK), BF16),
        in_specs=[IN_SMEM] + [IN_VMEM] * CHIPS,
        out_specs=IN_VMEM,
        scratch_shapes=[pltpu.VMEM((STORED, EQ, NTOK), F32)],
        compiler_params=params(),
        cost_estimate=cost(0, 3_000_000),
        name="collect",
    )(rows, *arrived)


def swap(x):
    return lax.ppermute(x, "seq", [(i, i ^ 1) for i in range(N_SEQ)])


def ahead(x, by):
    return lax.ppermute(x, "seq", [(i, (i + 2 * by) % N_SEQ) for i in range(N_SEQ)])


def after(x, *done):
    return lax.optimization_barrier((x,) + done)[0]


def exchange(messages):
    arrived = [messages[0]] + [None] * (CHIPS - 1)
    for by, behind in ((3, 0), (5, 0), (4, 0), (2, 0), (6, 0), (1, 3), (7, 5)):
        message = messages[by]
        if behind:
            message = after(message, arrived[behind])
        arrived[by] = ahead(message, by)
    return arrived


def turn(x, by):
    return lax.ppermute(x, "tp", [(i, (i + by) % N_TP) for i in range(N_TP)])


def section_back(x):
    count = lax.axis_size("section")
    return lax.ppermute(x, "section", [(i, i - 1) for i in range(1, count)])


def deliver_kernel(*refs):
    out_ref = refs[-1]
    at = 0
    for ref in refs[:-1]:
        rows = ref.shape[0]
        out_ref[at : at + rows] = ref[...]
        at += rows


def deliver(parts):
    return pl.pallas_call(
        deliver_kernel,
        out_shape=jax.ShapeDtypeStruct((TOKENS_DEV, WIDTH), BF16),
        in_specs=[IN_VMEM] * len(parts),
        out_specs=IN_VMEM,
        compiler_params=params(),
        cost_estimate=cost(0, 2_000_000),
        name="deliver",
    )(*parts)


def body(queries, encoded, neighbour, send_rows, key_weight, value_weight, ctx_grad):
    sources, rows = neighbour[0], send_rows[0, 0]
    kw, vw = key_weight[0], value_weight[0]
    share = take_share(encoded[0])
    sibling_sources = swap(sources)
    sibling_rows = after(swap(rows), sibling_sources)
    arrived = exchange(pack_rows(rows, sibling_rows, share, swap(share)))
    picked = pick(sources, arrived)
    low, high = turn(picked[0], 1), turn(picked[0], -1)
    own_first, own_second = project(picked, kw, vw)
    across = [turn(low[0], 1), turn(after(high, *own_first)[1], -1)]
    own = after(picked[1], low, high)
    others = [turn(own, -shift) for shift in range(1, N_TP)]
    next_first, last_first = project([high, low], kw, vw)
    both = tuple(range(HALVES))
    known = [
        [(0, own_first), (1, next_first), (3, last_first)],
        [(0, own_second)],
    ]
    raw = [
        [(2, (half,), x) for half, x in enumerate(across)],
        [(shift, both, x) for shift, x in enumerate(others, 1)],
    ]
    held = ()
    grads = []
    for group, (first, spans) in enumerate(GROUPS):
        *held, first_piece, second, third, fourth = attention(
            known[group], raw[group], kw, vw, queries[0], ctx_grad[0], first, spans, held
        )
        turned = [turn(x, by) for by, x in ((1, second), (2, third), (3, fourth))]
        grads.append(sum_parts([first_piece] + turned))
    context, query_grad = held
    passed = section_back(query_grad)
    messages = place(sources, sibling_sources, grads + [swap(grad) for grad in grads])
    returned = exchange(messages)
    encoded_grad = jnp.swapaxes(collect(rows, returned), 1, 2)
    passed = deliver([after(passed, returned[3])])
    return (context[None], passed[None], encoded_grad[None])


def solution(mesh):
    placed = (
        P("section", "seq", "tp"),
        P("section", "seq", None, None),
        P("section", "seq", None),
        P("section", "seq", None, None),
        P("section", None, "tp"),
        P("section", None, "tp"),
        P("section", "seq", "tp"),
    )
    return jax.shard_map(
        body,
        mesh=mesh,
        in_specs=placed,
        out_specs=(
            P("section", "seq", "tp"),
            P("section", "seq", "tp"),
            P("section", "seq", None, "tp"),
        ),
        check_vma=False,
    )
```

```python
import functools
import math

import jax
import jax.numpy as jnp
from jax import lax
from jax.experimental import pallas as pl
from jax.experimental.pallas import tpu as pltpu
from jax.sharding import PartitionSpec as P

DH = 128
E = 896
SPAN = 64
KNB = 2
NTOK = 128
N_SEQ = 16
CHIPS = N_SEQ // 2
CAP = 2
N_TP = 4
SLOTS = N_SEQ * CAP
REQ = 12
STORED = 16
SPANS_DEV = 6
TOKENS_DEV = SPANS_DEV * SPAN
HEADS_DEV = 8
WIDTH = HEADS_DEV * DH
PART = NTOK // N_TP
EQ = E // N_TP
KEYS = KNB * NTOK
GROUPS = ((0, 3), (3, 3))
HALVES = 2
ROWS = PART // HALVES
VMEM = 24 * 1024 * 1024
WIDE_VMEM = 60 * 1024 * 1024
BF16 = jnp.bfloat16
F32 = jnp.float32
SCALE = 1.0 / math.sqrt(DH)
IN_SMEM = pl.BlockSpec(memory_space=pltpu.SMEM)
IN_VMEM = pl.BlockSpec(memory_space=pltpu.VMEM)
ANYWHERE = pl.BlockSpec(memory_space=pl.ANY)


def params(limit=VMEM):
    return pltpu.CompilerParams(vmem_limit_bytes=limit)


def cost(flops, bytes_accessed):
    return pl.CostEstimate(flops=flops, bytes_accessed=bytes_accessed, transcendentals=0)


def dot(a, b):
    return jnp.dot(a, b, preferred_element_type=F32)


def dot_nt(a, b):
    return lax.dot_general(a, b, (((1,), (1,)), ((), ())), preferred_element_type=F32)


def dot_tn(a, b):
    return lax.dot_general(a, b, (((0,), (0,)), ((), ())), preferred_element_type=F32)


def member(shift):
    return lax.rem(lax.axis_index("tp") + shift, N_TP)


def share_kernel(encoded_ref, out_ref, sem):
    start = pl.multiple_of(lax.axis_index("tp") * PART, PART)
    copy = pltpu.make_async_copy(encoded_ref.at[:, pl.ds(start, PART)], out_ref, sem)
    copy.start()
    copy.wait()


def take_share(encoded):
    return pl.pallas_call(
        share_kernel,
        out_shape=jax.ShapeDtypeStruct((STORED, PART, E), BF16),
        in_specs=[ANYWHERE],
        out_specs=IN_VMEM,
        scratch_shapes=[pltpu.SemaphoreType.DMA],
        compiler_params=params(WIDE_VMEM),
        cost_estimate=cost(0, 2_000_000),
        name="take_share",
    )(encoded)


def pack_kernel(rows_ref, sibling_rows_ref, share_ref, sibling_ref, *outs):
    me = lax.axis_index("seq")
    chip, core = me // 2, lax.rem(me, 2)
    for ahead in range(CHIPS):
        device = lax.rem(chip + ahead, CHIPS) * 2 + core
        for j in range(CAP):
            row = jnp.clip(rows_ref[device, j], 0, STORED - 1)
            outs[ahead][j] = share_ref[row]
            row = jnp.clip(sibling_rows_ref[device, j], 0, STORED - 1)
            outs[ahead][CAP + j] = sibling_ref[row]


def pack_rows(rows, sibling_rows, share, sibling):
    return pl.pallas_call(
        pack_kernel,
        out_shape=[jax.ShapeDtypeStruct((2 * CAP, PART, E), BF16)] * CHIPS,
        in_specs=[IN_SMEM, IN_SMEM, IN_VMEM, IN_VMEM],
        out_specs=[IN_VMEM] * CHIPS,
        compiler_params=params(WIDE_VMEM),
        cost_estimate=cost(0, 3_000_000),
        name="pack_rows",
    )(rows, sibling_rows, share, sibling)


def places_of(neighbour_ref):
    me = lax.axis_index("seq")
    chip, core = me // 2, lax.rem(me, 2)
    sources = [neighbour_ref[r // KNB, r % KNB] for r in range(REQ)]
    places = []
    for r in range(REQ):
        earlier = jnp.int32(0)
        for q in range(r):
            earlier = earlier + (sources[q] == sources[r]).astype(jnp.int32)
        away = lax.rem(sources[r] // 2 - chip + CHIPS, CHIPS)
        other = (lax.rem(sources[r], 2) != core).astype(jnp.int32)
        places.append((away, other, jnp.minimum(earlier, CAP - 1)))
    return places


def pick_kernel(neighbour_ref, *refs):
    arrived, outs, table = refs[:CHIPS], refs[CHIPS:-1], refs[-1]
    for at in range(SLOTS):
        table[at] = REQ
    for r, (away, other, slot) in enumerate(places_of(neighbour_ref)):
        table[away * 2 * CAP + other * CAP + slot] = r
    half = GROUPS[0][1] * KNB
    for away in range(CHIPS):
        for block in range(2 * CAP):
            r = table[away * 2 * CAP + block]
            ref = arrived[(CHIPS - away) % CHIPS]

            @pl.when(r < half)
            def _():
                for n in range(HALVES):
                    outs[0][n, r] = ref[block, n * ROWS : (n + 1) * ROWS]

            @pl.when((r >= half) & (r < REQ))
            def _():
                for n in range(HALVES):
                    outs[1][n, r - half] = ref[block, n * ROWS : (n + 1) * ROWS]


def pick(neighbour, arrived):
    return pl.pallas_call(
        pick_kernel,
        out_shape=[
            jax.ShapeDtypeStruct((HALVES, spans * KNB, ROWS, E), BF16) for first, spans in GROUPS
        ],
        in_specs=[IN_SMEM] + [IN_VMEM] * CHIPS,
        out_specs=[IN_VMEM] * len(GROUPS),
        scratch_shapes=[pltpu.SMEM((SLOTS,), jnp.int32)],
        compiler_params=params(),
        cost_estimate=cost(0, 3_000_000),
        name="pick",
    )(neighbour, *arrived)


def attention_kernel(hops, *refs):
    pieces = refs[:hops]
    kw_ref, vw_ref, q_ref, g_ref = refs[hops : hops + 4]
    ctx_ref, qg_ref = refs[-(N_TP + 8) : -(N_TP + 6)]
    outs = refs[-(N_TP + 6) : -6]
    xs, ks, vs, kgs, vgs, backs = refs[-6:]
    step = pl.program_id(0)

    @pl.when(step == 0)
    def _():
        order = (0, 1, 2, 3) if hops == N_TP else (0, 1, 2, 2, 3)
        for n, shift in enumerate(order):
            ref = pieces[n]
            halves = [n - 2] if len(ref.shape) == 3 else range(HALVES)
            for half in halves:
                begin = pl.multiple_of(member(shift) * PART + half * ROWS, ROWS)
                for r in range(ref.shape[-3]):
                    piece = ref[r] if len(ref.shape) == 3 else ref[half, r]
                    xs[r, pl.ds(begin, ROWS), :] = piece
        x = xs[...].reshape(-1, E)
        ks[...] = dot(x, kw_ref[...]).astype(BF16)
        vs[...] = dot(x, vw_ref[...]).astype(BF16)

    mine = pl.ds(pl.multiple_of(step * KEYS, KEYS), KEYS)
    cols = [slice(h * DH, (h + 1) * DH) for h in range(HEADS_DEV)]
    scores = [dot_nt(q_ref[:, c], ks[mine, c]) for c in cols]
    prob_grads = [dot_nt(g_ref[:, c], vs[mine, c]) for c in cols]
    lows, dscores = [], []
    for score, prob_grad in zip(scores, prob_grads):
        exponent = jnp.exp(score * SCALE)
        probs = exponent / jnp.sum(exponent, axis=-1, keepdims=True)
        delta = jnp.sum(probs * prob_grad, axis=-1, keepdims=True)
        lows.append(probs.astype(BF16))
        dscores.append((probs * (prob_grad - delta) * SCALE).astype(BF16))
    for c, low, dscore in zip(cols, lows, dscores):
        kgs[c, :] = dot_tn(q_ref[:, c], dscore).astype(BF16)
        vgs[c, :] = dot_tn(g_ref[:, c], low).astype(BF16)
    for c, low, dscore in zip(cols, lows, dscores):
        ctx_ref[:, c] = dot(low, vs[mine, c]).astype(BF16)
        qg_ref[:, c] = dot(dscore, ks[mine, c]).astype(BF16)
    backs[...] = (dot(kw_ref[...], kgs[...]) + dot(vw_ref[...], vgs[...])).astype(BF16)
    for shift in range(N_TP):
        begin = pl.multiple_of(member(shift) * EQ, 16)
        for k in range(KNB):
            outs[shift][k] = backs[pl.ds(begin, EQ), k * NTOK : (k + 1) * NTOK]


def attention(pieces, kw, vw, queries, ctx_grad, first, spans, held):
    whole = pl.BlockSpec((E, WIDTH), lambda c: (0, 0))
    span = pl.BlockSpec((SPAN, WIDTH), lambda c: (c + first, 0))
    back = pl.BlockSpec((KNB, EQ, NTOK), lambda c: (c, 0, 0))
    wide = jax.ShapeDtypeStruct((TOKENS_DEV, WIDTH), BF16)
    piece = jax.ShapeDtypeStruct((spans * KNB, EQ, NTOK), BF16)
    hops = len(pieces)
    return pl.pallas_call(
        functools.partial(attention_kernel, hops),
        grid=(spans,),
        out_shape=[wide, wide] + [piece] * N_TP,
        in_specs=[IN_VMEM] * hops + [whole, whole, span, span] + [ANYWHERE] * len(held),
        out_specs=[span, span] + [back] * N_TP,
        scratch_shapes=[
            pltpu.VMEM((spans * KNB, NTOK, E), BF16),
            pltpu.VMEM((spans * KEYS, WIDTH), BF16),
            pltpu.VMEM((spans * KEYS, WIDTH), BF16),
            pltpu.VMEM((WIDTH, KEYS), BF16),
            pltpu.VMEM((WIDTH, KEYS), BF16),
            pltpu.VMEM((E, KEYS), BF16),
        ],
        input_output_aliases={hops + 4 + i: i for i in range(len(held))},
        compiler_params=params(),
        cost_estimate=cost(spans * 2_200_000_000, 5_000_000 + spans * 1_500_000),
        name="attention",
    )(*pieces, kw, vw, queries, ctx_grad, *held)


def sum_kernel(*refs):
    out_ref = refs[-1]
    for r in range(out_ref.shape[0]):
        total = refs[0][r].astype(F32)
        for part in refs[1:-1]:
            total = total + part[r].astype(F32)
        out_ref[r] = total.astype(BF16)


def sum_parts(parts):
    return pl.pallas_call(
        sum_kernel,
        out_shape=jax.ShapeDtypeStruct(parts[0].shape, BF16),
        in_specs=[IN_VMEM] * len(parts),
        out_specs=IN_VMEM,
        compiler_params=params(),
        cost_estimate=cost(0, 2_000_000),
        name="sum_parts",
    )(*parts)


def place_kernel(neighbour_ref, sibling_neighbour_ref, *refs):
    grads, outs, table = refs[:4], refs[4:-1], refs[-1]
    half = GROUPS[0][1] * KNB
    for at in range(SLOTS):
        table[at] = REQ
    for whose, ref in enumerate((neighbour_ref, sibling_neighbour_ref)):
        for r, (away, other, slot) in enumerate(places_of(ref)):
            at = away * 2 * CAP + whose * CAP + slot

            @pl.when(other == 0)
            def _():
                table[at] = r

    for away in range(CHIPS):
        for block in range(2 * CAP):
            r = table[away * 2 * CAP + block]
            low, high = grads[2 * (block // CAP)], grads[2 * (block // CAP) + 1]
            out = outs[away]

            @pl.when(r < half)
            def _():
                out[block] = low[r]

            @pl.when((r >= half) & (r < REQ))
            def _():
                out[block] = high[r - half]

            @pl.when(r >= REQ)
            def _():
                out[block] = jnp.zeros((EQ, NTOK), BF16)


def place(neighbour, sibling_neighbour, grads):
    return pl.pallas_call(
        place_kernel,
        out_shape=[jax.ShapeDtypeStruct((2 * CAP, EQ, NTOK), BF16)] * CHIPS,
        in_specs=[IN_SMEM, IN_SMEM] + [IN_VMEM] * len(grads),
        out_specs=[IN_VMEM] * CHIPS,
        scratch_shapes=[pltpu.SMEM((SLOTS,), jnp.int32)],
        compiler_params=params(),
        cost_estimate=cost(0, 3_000_000),
        name="place",
    )(neighbour, sibling_neighbour, *grads)


def collect_kernel(rows_ref, *refs):
    arrived, (out_ref, acc) = refs[:CHIPS], refs[CHIPS:]
    me = lax.axis_index("seq")
    chip, core = me // 2, lax.rem(me, 2)
    acc[...] = jnp.zeros(acc.shape, F32)
    for behind in range(CHIPS):
        device = lax.rem(chip - behind + CHIPS, CHIPS) * 2
        for block in range(2 * CAP):
            requester = device + (core if block < CAP else 1 - core)
            row = jnp.clip(rows_ref[requester, block % CAP], 0, STORED - 1)
            acc[row] += arrived[behind][block].astype(F32)
    out_ref[...] = acc[...].astype(BF16)


def collect(rows, arrived):
    return pl.pallas_call(
        collect_kernel,
        out_shape=jax.ShapeDtypeStruct((STORED, EQ, NTOK), BF16),
        in_specs=[IN_SMEM] + [IN_VMEM] * CHIPS,
        out_specs=IN_VMEM,
        scratch_shapes=[pltpu.VMEM((STORED, EQ, NTOK), F32)],
        compiler_params=params(),
        cost_estimate=cost(0, 3_000_000),
        name="collect",
    )(rows, *arrived)


def swap(x):
    return lax.ppermute(x, "seq", [(i, i ^ 1) for i in range(N_SEQ)])


def ahead(x, by):
    return lax.ppermute(x, "seq", [(i, (i + 2 * by) % N_SEQ) for i in range(N_SEQ)])


def after(x, *done):
    return lax.optimization_barrier((x,) + done)[0]


def exchange(messages):
    arrived = [messages[0]] + [None] * (CHIPS - 1)
    for by, behind in ((3, 0), (5, 0), (4, 0), (2, 0), (6, 0), (1, 3), (7, 5)):
        message = messages[by]
        if behind:
            message = after(message, arrived[behind])
        arrived[by] = ahead(message, by)
    return arrived


def turn(x, by):
    return lax.ppermute(x, "tp", [(i, (i + by) % N_TP) for i in range(N_TP)])


def section_back(x):
    count = lax.axis_size("section")
    return lax.ppermute(x, "section", [(i, i - 1) for i in range(1, count)])


def deliver_kernel(*refs):
    out_ref = refs[-1]
    at = 0
    for ref in refs[:-1]:
        rows = ref.shape[0]
        out_ref[at : at + rows] = ref[...]
        at += rows


def deliver(parts):
    return pl.pallas_call(
        deliver_kernel,
        out_shape=jax.ShapeDtypeStruct((TOKENS_DEV, WIDTH), BF16),
        in_specs=[IN_VMEM] * len(parts),
        out_specs=IN_VMEM,
        compiler_params=params(),
        cost_estimate=cost(0, 2_000_000),
        name="deliver",
    )(*parts)


def body(queries, encoded, neighbour, send_rows, key_weight, value_weight, ctx_grad):
    sources, rows = neighbour[0], send_rows[0, 0]
    kw, vw = key_weight[0], value_weight[0]
    share = take_share(encoded[0])
    sibling_sources = swap(sources)
    sibling_rows = after(swap(rows), sibling_sources)
    arrived = exchange(pack_rows(rows, sibling_rows, share, swap(share)))
    picked = pick(sources, arrived)
    low, high = turn(picked[0], 1), turn(picked[0], -1)
    across = [turn(low[0], 1), turn(high[1], -1)]
    whole = [[picked[0], high] + across + [low]]
    own = after(picked[1], low, high, across[0])
    whole.append([own] + [turn(own, -shift) for shift in range(1, N_TP)])
    held = ()
    grads = []
    for group, (first, spans) in enumerate(GROUPS):
        *held, first_piece, second, third, fourth = attention(
            whole[group], kw, vw, queries[0], ctx_grad[0], first, spans, held
        )
        turned = [turn(x, by) for by, x in ((1, second), (2, third), (3, fourth))]
        grads.append(sum_parts([first_piece] + turned))
    context, query_grad = held
    passed = section_back(query_grad)
    messages = place(sources, sibling_sources, grads + [swap(grad) for grad in grads])
    returned = exchange(messages)
    encoded_grad = jnp.swapaxes(collect(rows, returned), 1, 2)
    passed = deliver([after(passed, returned[3])])
    return (context[None], passed[None], encoded_grad[None])


def solution(mesh):
    placed = (
        P("section", "seq", "tp"),
        P("section", "seq", None, None),
        P("section", "seq", None),
        P("section", "seq", None, None),
        P("section", None, "tp"),
        P("section", None, "tp"),
        P("section", "seq", "tp"),
    )
    return jax.shard_map(
        body,
        mesh=mesh,
        in_specs=placed,
        out_specs=(
            P("section", "seq", "tp"),
            P("section", "seq", "tp"),
            P("section", "seq", None, "tp"),
        ),
        check_vma=False,
    )
```

```python
import functools
import math

import jax
import jax.numpy as jnp
from jax import lax
from jax.experimental import pallas as pl
from jax.experimental.pallas import tpu as pltpu
from jax.sharding import PartitionSpec as P

DH = 128
E = 896
SPAN = 64
KNB = 2
NTOK = 128
N_SEQ = 16
CHIPS = N_SEQ // 2
ACROSS = CHIPS // 2
SENT = tuple(by for by in range(CHIPS) if by != ACROSS)
CAP = 2
N_TP = 4
SLOTS = N_SEQ * CAP
REQ = 12
STORED = 16
SPANS_DEV = 6
TOKENS_DEV = SPANS_DEV * SPAN
HEADS_DEV = 8
WIDTH = HEADS_DEV * DH
PART = NTOK // N_TP
EQ = E // N_TP
KEYS = KNB * NTOK
GROUPS = ((0, 3), (3, 3))
HALVES = 2
ROWS = PART // HALVES
VMEM = 24 * 1024 * 1024
WIDE_VMEM = 60 * 1024 * 1024
BF16 = jnp.bfloat16
F32 = jnp.float32
SCALE = 1.0 / math.sqrt(DH)
IN_SMEM = pl.BlockSpec(memory_space=pltpu.SMEM)
IN_VMEM = pl.BlockSpec(memory_space=pltpu.VMEM)
ANYWHERE = pl.BlockSpec(memory_space=pl.ANY)


def params(limit=VMEM):
    return pltpu.CompilerParams(vmem_limit_bytes=limit)


def cost(flops, bytes_accessed):
    return pl.CostEstimate(flops=flops, bytes_accessed=bytes_accessed, transcendentals=0)


def dot(a, b):
    return jnp.dot(a, b, preferred_element_type=F32)


def dot_nt(a, b):
    return lax.dot_general(a, b, (((1,), (1,)), ((), ())), preferred_element_type=F32)


def dot_tn(a, b):
    return lax.dot_general(a, b, (((0,), (0,)), ((), ())), preferred_element_type=F32)


def member(shift):
    return lax.rem(lax.axis_index("tp") + shift, N_TP)


def share_kernel(encoded_ref, out_ref, sem):
    start = pl.multiple_of(lax.axis_index("tp") * PART, PART)
    copy = pltpu.make_async_copy(encoded_ref.at[:, pl.ds(start, PART)], out_ref, sem)
    copy.start()
    copy.wait()


def take_share(encoded):
    return pl.pallas_call(
        share_kernel,
        out_shape=jax.ShapeDtypeStruct((STORED, PART, E), BF16),
        in_specs=[ANYWHERE],
        out_specs=IN_VMEM,
        scratch_shapes=[pltpu.SemaphoreType.DMA],
        compiler_params=params(WIDE_VMEM),
        cost_estimate=cost(0, 2_000_000),
        name="take_share",
    )(encoded)


def message_blocks(by):
    return 3 * CAP if by in (1, CHIPS - 1) else 2 * CAP


def outgoing(refs, by, block):
    if len(refs) == CHIPS:
        return refs[by].at[block]
    if by != ACROSS:
        return refs[SENT.index(by)].at[block]
    relay = 1 if block < CAP else CHIPS - 1
    return refs[SENT.index(relay)].at[2 * CAP + block % CAP]


def incoming(refs, by, block):
    if len(refs) == CHIPS:
        return refs[by].at[block]
    if by != ACROSS:
        return refs[SENT.index(by)].at[block]
    return refs[len(SENT) + block // CAP].at[block % CAP]


def pack_kernel(rows_ref, sibling_rows_ref, share_ref, sibling_ref, *outs):
    me = lax.axis_index("seq")
    chip, core = me // 2, lax.rem(me, 2)
    for ahead in range(CHIPS):
        device = lax.rem(chip + ahead, CHIPS) * 2 + core
        for j in range(CAP):
            row = jnp.clip(rows_ref[device, j], 0, STORED - 1)
            outgoing(outs, ahead, j)[...] = share_ref[row]
            row = jnp.clip(sibling_rows_ref[device, j], 0, STORED - 1)
            outgoing(outs, ahead, CAP + j)[...] = sibling_ref[row]


def pack_rows(rows, sibling_rows, share, sibling):
    return pl.pallas_call(
        pack_kernel,
        out_shape=[jax.ShapeDtypeStruct((message_blocks(by), PART, E), BF16) for by in SENT],
        in_specs=[IN_SMEM, IN_SMEM, IN_VMEM, IN_VMEM],
        out_specs=[IN_VMEM] * len(SENT),
        compiler_params=params(WIDE_VMEM),
        cost_estimate=cost(0, 3_000_000),
        name="pack_rows",
    )(rows, sibling_rows, share, sibling)


def places_of(neighbour_ref):
    me = lax.axis_index("seq")
    chip, core = me // 2, lax.rem(me, 2)
    sources = [neighbour_ref[r // KNB, r % KNB] for r in range(REQ)]
    places = []
    for r in range(REQ):
        earlier = jnp.int32(0)
        for q in range(r):
            earlier = earlier + (sources[q] == sources[r]).astype(jnp.int32)
        away = lax.rem(sources[r] // 2 - chip + CHIPS, CHIPS)
        other = (lax.rem(sources[r], 2) != core).astype(jnp.int32)
        places.append((away, other, jnp.minimum(earlier, CAP - 1)))
    return places


def pick_kernel(neighbour_ref, *refs):
    count = len(SENT) + 2
    arrived, outs, table = refs[:count], refs[count:-1], refs[-1]
    for at in range(SLOTS):
        table[at] = REQ
    for r, (away, other, slot) in enumerate(places_of(neighbour_ref)):
        table[away * 2 * CAP + other * CAP + slot] = r
    half = GROUPS[0][1] * KNB
    for away in range(CHIPS):
        for block in range(2 * CAP):
            r = table[away * 2 * CAP + block]
            ref = incoming(arrived, (CHIPS - away) % CHIPS, block)

            @pl.when(r < half)
            def _():
                for n in range(HALVES):
                    outs[0][n, r] = ref[n * ROWS : (n + 1) * ROWS]

            @pl.when((r >= half) & (r < REQ))
            def _():
                for n in range(HALVES):
                    outs[1][n, r - half] = ref[n * ROWS : (n + 1) * ROWS]


def pick(neighbour, arrived):
    return pl.pallas_call(
        pick_kernel,
        out_shape=[
            jax.ShapeDtypeStruct((HALVES, spans * KNB, ROWS, E), BF16) for first, spans in GROUPS
        ],
        in_specs=[IN_SMEM] + [IN_VMEM] * len(arrived),
        out_specs=[IN_VMEM] * len(GROUPS),
        scratch_shapes=[pltpu.SMEM((SLOTS,), jnp.int32)],
        compiler_params=params(),
        cost_estimate=cost(0, 3_000_000),
        name="pick",
    )(neighbour, *arrived)


def attention_kernel(hops, *refs):
    pieces = refs[:hops]
    kw_ref, vw_ref, q_ref, g_ref = refs[hops : hops + 4]
    ctx_ref, qg_ref = refs[-(N_TP + 8) : -(N_TP + 6)]
    outs = refs[-(N_TP + 6) : -6]
    xs, ks, vs, kgs, vgs, backs = refs[-6:]
    step = pl.program_id(0)

    @pl.when(step == 0)
    def _():
        order = (0, 1, 2, 3) if hops == N_TP else (0, 1, 2, 2, 3)
        for n, shift in enumerate(order):
            ref = pieces[n]
            halves = [n - 2] if len(ref.shape) == 3 else range(HALVES)
            for half in halves:
                begin = pl.multiple_of(member(shift) * PART + half * ROWS, ROWS)
                for r in range(ref.shape[-3]):
                    piece = ref[r] if len(ref.shape) == 3 else ref[half, r]
                    xs[r, pl.ds(begin, ROWS), :] = piece
        x = xs[...].reshape(-1, E)
        ks[...] = dot(x, kw_ref[...]).astype(BF16)
        vs[...] = dot(x, vw_ref[...]).astype(BF16)

    mine = pl.ds(pl.multiple_of(step * KEYS, KEYS), KEYS)
    cols = [slice(h * DH, (h + 1) * DH) for h in range(HEADS_DEV)]
    scores = [dot_nt(q_ref[:, c], ks[mine, c]) for c in cols]
    prob_grads = [dot_nt(g_ref[:, c], vs[mine, c]) for c in cols]
    lows, dscores = [], []
    for score, prob_grad in zip(scores, prob_grads):
        exponent = jnp.exp(score * SCALE)
        probs = exponent / jnp.sum(exponent, axis=-1, keepdims=True)
        delta = jnp.sum(probs * prob_grad, axis=-1, keepdims=True)
        lows.append(probs.astype(BF16))
        dscores.append((probs * (prob_grad - delta) * SCALE).astype(BF16))
    for c, low, dscore in zip(cols, lows, dscores):
        kgs[c, :] = dot_tn(q_ref[:, c], dscore).astype(BF16)
        vgs[c, :] = dot_tn(g_ref[:, c], low).astype(BF16)
    for c, low, dscore in zip(cols, lows, dscores):
        ctx_ref[:, c] = dot(low, vs[mine, c]).astype(BF16)
        qg_ref[:, c] = dot(dscore, ks[mine, c]).astype(BF16)
    backs[...] = (dot(kw_ref[...], kgs[...]) + dot(vw_ref[...], vgs[...])).astype(BF16)
    for shift in range(N_TP):
        begin = pl.multiple_of(member(shift) * EQ, 16)
        for k in range(KNB):
            outs[shift][k] = backs[pl.ds(begin, EQ), k * NTOK : (k + 1) * NTOK]


def attention(pieces, kw, vw, queries, ctx_grad, first, spans, held):
    whole = pl.BlockSpec((E, WIDTH), lambda c: (0, 0))
    span = pl.BlockSpec((SPAN, WIDTH), lambda c: (c + first, 0))
    back = pl.BlockSpec((KNB, EQ, NTOK), lambda c: (c, 0, 0))
    wide = jax.ShapeDtypeStruct((TOKENS_DEV, WIDTH), BF16)
    piece = jax.ShapeDtypeStruct((spans * KNB, EQ, NTOK), BF16)
    hops = len(pieces)
    return pl.pallas_call(
        functools.partial(attention_kernel, hops),
        grid=(spans,),
        out_shape=[wide, wide] + [piece] * N_TP,
        in_specs=[IN_VMEM] * hops + [whole, whole, span, span] + [ANYWHERE] * len(held),
        out_specs=[span, span] + [back] * N_TP,
        scratch_shapes=[
            pltpu.VMEM((spans * KNB, NTOK, E), BF16),
            pltpu.VMEM((spans * KEYS, WIDTH), BF16),
            pltpu.VMEM((spans * KEYS, WIDTH), BF16),
            pltpu.VMEM((WIDTH, KEYS), BF16),
            pltpu.VMEM((WIDTH, KEYS), BF16),
            pltpu.VMEM((E, KEYS), BF16),
        ],
        input_output_aliases={hops + 4 + i: i for i in range(len(held))},
        compiler_params=params(),
        cost_estimate=cost(spans * 2_200_000_000, 5_000_000 + spans * 1_500_000),
        name="attention",
    )(*pieces, kw, vw, queries, ctx_grad, *held)


def sum_kernel(*refs):
    out_ref = refs[-1]
    for r in range(out_ref.shape[0]):
        total = refs[0][r].astype(F32)
        for part in refs[1:-1]:
            total = total + part[r].astype(F32)
        out_ref[r] = total.astype(BF16)


def sum_parts(parts):
    return pl.pallas_call(
        sum_kernel,
        out_shape=jax.ShapeDtypeStruct(parts[0].shape, BF16),
        in_specs=[IN_VMEM] * len(parts),
        out_specs=IN_VMEM,
        compiler_params=params(),
        cost_estimate=cost(0, 2_000_000),
        name="sum_parts",
    )(*parts)


def place_kernel(neighbour_ref, sibling_neighbour_ref, *refs):
    grads, outs, table = refs[:4], refs[4:-1], refs[-1]
    half = GROUPS[0][1] * KNB
    for at in range(SLOTS):
        table[at] = REQ
    for whose, ref in enumerate((neighbour_ref, sibling_neighbour_ref)):
        for r, (away, other, slot) in enumerate(places_of(ref)):
            at = away * 2 * CAP + whose * CAP + slot

            @pl.when(other == 0)
            def _():
                table[at] = r

    for away in range(CHIPS):
        for block in range(2 * CAP):
            r = table[away * 2 * CAP + block]
            low, high = grads[2 * (block // CAP)], grads[2 * (block // CAP) + 1]
            out = outgoing(outs, away, block)

            @pl.when(r < half)
            def _():
                out[...] = low[r]

            @pl.when((r >= half) & (r < REQ))
            def _():
                out[...] = high[r - half]

            @pl.when(r >= REQ)
            def _():
                out[...] = jnp.zeros((EQ, NTOK), BF16)


def place(neighbour, sibling_neighbour, grads):
    return pl.pallas_call(
        place_kernel,
        out_shape=[jax.ShapeDtypeStruct((2 * CAP, EQ, NTOK), BF16)] * CHIPS,
        in_specs=[IN_SMEM, IN_SMEM] + [IN_VMEM] * len(grads),
        out_specs=[IN_VMEM] * CHIPS,
        scratch_shapes=[pltpu.SMEM((SLOTS,), jnp.int32)],
        compiler_params=params(),
        cost_estimate=cost(0, 3_000_000),
        name="place",
    )(neighbour, sibling_neighbour, *grads)


def collect_kernel(rows_ref, *refs):
    arrived, (out_ref, acc) = refs[:-2], refs[-2:]
    me = lax.axis_index("seq")
    chip, core = me // 2, lax.rem(me, 2)
    acc[...] = jnp.zeros(acc.shape, F32)
    for behind in range(CHIPS):
        device = lax.rem(chip - behind + CHIPS, CHIPS) * 2
        for block in range(2 * CAP):
            requester = device + (core if block < CAP else 1 - core)
            row = jnp.clip(rows_ref[requester, block % CAP], 0, STORED - 1)
            acc[row] += incoming(arrived, behind, block)[...].astype(F32)
    out_ref[...] = acc[...].astype(BF16)


def collect(rows, arrived):
    return pl.pallas_call(
        collect_kernel,
        out_shape=jax.ShapeDtypeStruct((STORED, EQ, NTOK), BF16),
        in_specs=[IN_SMEM] + [IN_VMEM] * len(arrived),
        out_specs=IN_VMEM,
        scratch_shapes=[pltpu.VMEM((STORED, EQ, NTOK), F32)],
        compiler_params=params(),
        cost_estimate=cost(0, 3_000_000),
        name="collect",
    )(rows, *arrived)


def swap(x):
    return lax.ppermute(x, "seq", [(i, i ^ 1) for i in range(N_SEQ)])


def ahead(x, by):
    return lax.ppermute(x, "seq", [(i, (i + 2 * by) % N_SEQ) for i in range(N_SEQ)])


def after(x, *done):
    return lax.optimization_barrier((x,) + done)[0]


def exchange_relayed(messages):
    local, right, *middle, left = messages
    right, left = ahead(right, 1), ahead(left, CHIPS - 1)
    middle = [ahead(x, by) for x, by in zip(middle, SENT[2:-1])]
    first = ahead(right[2 * CAP :], ACROSS - 1)
    second = ahead(left[2 * CAP :], ACROSS + 1)
    return [local, right, *middle, left, first, second]


def exchange(messages):
    arrived = [messages[0]] + [None] * (CHIPS - 1)
    for by, behind in ((3, 0), (5, 0), (4, 0), (2, 0), (6, 0), (1, 3), (7, 5)):
        message = messages[by]
        if behind:
            message = after(message, arrived[behind])
        arrived[by] = ahead(message, by)
    return arrived


def turn(x, by):
    return lax.ppermute(x, "tp", [(i, (i + by) % N_TP) for i in range(N_TP)])


def section_back(x):
    count = lax.axis_size("section")
    return lax.ppermute(x, "section", [(i, i - 1) for i in range(1, count)])


def deliver_kernel(*refs):
    out_ref = refs[-1]
    at = 0
    for ref in refs[:-1]:
        rows = ref.shape[0]
        out_ref[at : at + rows] = ref[...]
        at += rows


def deliver(parts):
    return pl.pallas_call(
        deliver_kernel,
        out_shape=jax.ShapeDtypeStruct((TOKENS_DEV, WIDTH), BF16),
        in_specs=[IN_VMEM] * len(parts),
        out_specs=IN_VMEM,
        compiler_params=params(),
        cost_estimate=cost(0, 2_000_000),
        name="deliver",
    )(*parts)


def body(queries, encoded, neighbour, send_rows, key_weight, value_weight, ctx_grad):
    sources, rows = neighbour[0], send_rows[0, 0]
    kw, vw = key_weight[0], value_weight[0]
    share = take_share(encoded[0])
    sibling_sources = swap(sources)
    sibling_rows = after(swap(rows), sibling_sources)
    arrived = exchange_relayed(pack_rows(rows, sibling_rows, share, swap(share)))
    picked = pick(sources, arrived)
    low, high = turn(picked[0], 1), turn(picked[0], -1)
    across = [turn(low[0], 1), turn(high[1], -1)]
    whole = [[picked[0], high] + across + [low]]
    own = after(picked[1], low, high, across[0])
    whole.append([own] + [turn(own, -shift) for shift in range(1, N_TP)])
    held = ()
    grads = []
    for group, (first, spans) in enumerate(GROUPS):
        *held, first_piece, second, third, fourth = attention(
            whole[group], kw, vw, queries[0], ctx_grad[0], first, spans, held
        )
        turned = [turn(x, by) for by, x in ((1, second), (2, third), (3, fourth))]
        grads.append(sum_parts([first_piece] + turned))
    context, query_grad = held
    passed = section_back(query_grad)
    messages = place(sources, sibling_sources, grads + [swap(grad) for grad in grads])
    returned = exchange(messages)
    encoded_grad = jnp.swapaxes(collect(rows, returned), 1, 2)
    passed = deliver([after(passed, returned[3])])
    return (context[None], passed[None], encoded_grad[None])


def solution(mesh):
    placed = (
        P("section", "seq", "tp"),
        P("section", "seq", None, None),
        P("section", "seq", None),
        P("section", "seq", None, None),
        P("section", None, "tp"),
        P("section", None, "tp"),
        P("section", "seq", "tp"),
    )
    return jax.shard_map(
        body,
        mesh=mesh,
        in_specs=placed,
        out_specs=(
            P("section", "seq", "tp"),
            P("section", "seq", "tp"),
            P("section", "seq", None, "tp"),
        ),
        check_vma=False,
    )
```

```python
import functools
import math

import jax
import jax.numpy as jnp
from jax import lax
from jax.experimental import pallas as pl
from jax.experimental.pallas import tpu as pltpu
from jax.sharding import PartitionSpec as P

DH = 128
E = 896
SPAN = 64
KNB = 2
NTOK = 128
N_SEQ = 16
CHIPS = N_SEQ // 2
ACROSS = CHIPS // 2
SENT = tuple(by for by in range(CHIPS) if by != ACROSS)
CAP = 2
N_TP = 4
SLOTS = N_SEQ * CAP
REQ = 12
STORED = 16
SPANS_DEV = 6
TOKENS_DEV = SPANS_DEV * SPAN
HEADS_DEV = 8
WIDTH = HEADS_DEV * DH
PART = NTOK // N_TP
EQ = E // N_TP
KEYS = KNB * NTOK
GROUPS = ((0, 3), (3, 3))
HALVES = 2
ROWS = PART // HALVES
VMEM = 24 * 1024 * 1024
WIDE_VMEM = 60 * 1024 * 1024
BF16 = jnp.bfloat16
F32 = jnp.float32
SCALE = 1.0 / math.sqrt(DH)
IN_SMEM = pl.BlockSpec(memory_space=pltpu.SMEM)
IN_VMEM = pl.BlockSpec(memory_space=pltpu.VMEM)
ANYWHERE = pl.BlockSpec(memory_space=pl.ANY)


def params(limit=VMEM):
    return pltpu.CompilerParams(vmem_limit_bytes=limit)


def cost(flops, bytes_accessed):
    return pl.CostEstimate(flops=flops, bytes_accessed=bytes_accessed, transcendentals=0)


def dot(a, b):
    return jnp.dot(a, b, preferred_element_type=F32)


def dot_nt(a, b):
    return lax.dot_general(a, b, (((1,), (1,)), ((), ())), preferred_element_type=F32)


def dot_tn(a, b):
    return lax.dot_general(a, b, (((0,), (0,)), ((), ())), preferred_element_type=F32)


def member(shift):
    return lax.rem(lax.axis_index("tp") + shift, N_TP)


def share_kernel(encoded_ref, out_ref, sem):
    start = pl.multiple_of(lax.axis_index("tp") * PART, PART)
    copy = pltpu.make_async_copy(encoded_ref.at[:, pl.ds(start, PART)], out_ref, sem)
    copy.start()
    copy.wait()


def take_share(encoded):
    return pl.pallas_call(
        share_kernel,
        out_shape=jax.ShapeDtypeStruct((STORED, PART, E), BF16),
        in_specs=[ANYWHERE],
        out_specs=IN_VMEM,
        scratch_shapes=[pltpu.SemaphoreType.DMA],
        compiler_params=params(WIDE_VMEM),
        cost_estimate=cost(0, 2_000_000),
        name="take_share",
    )(encoded)


def message_blocks(by):
    return 3 * CAP if by in (1, CHIPS - 1) else 2 * CAP


def outgoing(refs, by, block):
    if len(refs) == CHIPS:
        return refs[by].at[block]
    if by != ACROSS:
        return refs[SENT.index(by)].at[block]
    relay = 1 if block < CAP else CHIPS - 1
    return refs[SENT.index(relay)].at[2 * CAP + block % CAP]


def incoming(refs, by, block):
    if len(refs) == CHIPS:
        return refs[by].at[block]
    if by != ACROSS:
        return refs[SENT.index(by)].at[block]
    return refs[len(SENT) + block // CAP].at[block % CAP]


def pack_kernel(rows_ref, sibling_rows_ref, share_ref, sibling_ref, *outs):
    me = lax.axis_index("seq")
    chip, core = me // 2, lax.rem(me, 2)
    for ahead in range(CHIPS):
        device = lax.rem(chip + ahead, CHIPS) * 2 + core
        for j in range(CAP):
            row = jnp.clip(rows_ref[device, j], 0, STORED - 1)
            outgoing(outs, ahead, j)[...] = share_ref[row]
            row = jnp.clip(sibling_rows_ref[device, j], 0, STORED - 1)
            outgoing(outs, ahead, CAP + j)[...] = sibling_ref[row]


def pack_rows(rows, sibling_rows, share, sibling):
    return pl.pallas_call(
        pack_kernel,
        out_shape=[jax.ShapeDtypeStruct((message_blocks(by), PART, E), BF16) for by in SENT],
        in_specs=[IN_SMEM, IN_SMEM, IN_VMEM, IN_VMEM],
        out_specs=[IN_VMEM] * len(SENT),
        compiler_params=params(WIDE_VMEM),
        cost_estimate=cost(0, 3_000_000),
        name="pack_rows",
    )(rows, sibling_rows, share, sibling)


def places_of(neighbour_ref):
    me = lax.axis_index("seq")
    chip, core = me // 2, lax.rem(me, 2)
    sources = [neighbour_ref[r // KNB, r % KNB] for r in range(REQ)]
    places = []
    for r in range(REQ):
        earlier = jnp.int32(0)
        for q in range(r):
            earlier = earlier + (sources[q] == sources[r]).astype(jnp.int32)
        away = lax.rem(sources[r] // 2 - chip + CHIPS, CHIPS)
        other = (lax.rem(sources[r], 2) != core).astype(jnp.int32)
        places.append((away, other, jnp.minimum(earlier, CAP - 1)))
    return places


def pick_kernel(neighbour_ref, *refs):
    count = len(SENT) + 2
    arrived, outs, table = refs[:count], refs[count:-1], refs[-1]
    for at in range(SLOTS):
        table[at] = REQ
    for r, (away, other, slot) in enumerate(places_of(neighbour_ref)):
        table[away * 2 * CAP + other * CAP + slot] = r
    half = GROUPS[0][1] * KNB
    for away in range(CHIPS):
        for block in range(2 * CAP):
            r = table[away * 2 * CAP + block]
            ref = incoming(arrived, (CHIPS - away) % CHIPS, block)

            @pl.when(r < half)
            def _():
                for n in range(HALVES):
                    outs[0][n, r] = ref[n * ROWS : (n + 1) * ROWS]

            @pl.when((r >= half) & (r < REQ))
            def _():
                for n in range(HALVES):
                    outs[1][n, r - half] = ref[n * ROWS : (n + 1) * ROWS]


def pick(neighbour, arrived):
    return pl.pallas_call(
        pick_kernel,
        out_shape=[
            jax.ShapeDtypeStruct((HALVES, spans * KNB, ROWS, E), BF16) for first, spans in GROUPS
        ],
        in_specs=[IN_SMEM] + [IN_VMEM] * len(arrived),
        out_specs=[IN_VMEM] * len(GROUPS),
        scratch_shapes=[pltpu.SMEM((SLOTS,), jnp.int32)],
        compiler_params=params(),
        cost_estimate=cost(0, 3_000_000),
        name="pick",
    )(neighbour, *arrived)


def attention_kernel(hops, *refs):
    pieces = refs[:hops]
    kw_ref, vw_ref, q_ref, g_ref = refs[hops : hops + 4]
    ctx_ref, qg_ref = refs[-(N_TP + 8) : -(N_TP + 6)]
    outs = refs[-(N_TP + 6) : -6]
    xs, ks, vs, kgs, vgs, backs = refs[-6:]
    step = pl.program_id(0)

    @pl.when(step == 0)
    def _():
        order = (0, 1, 2, 3) if hops == N_TP else (0, 1, 2, 2, 3)
        for n, shift in enumerate(order):
            ref = pieces[n]
            halves = [n - 2] if len(ref.shape) == 3 else range(HALVES)
            for half in halves:
                begin = pl.multiple_of(member(shift) * PART + half * ROWS, ROWS)
                for r in range(ref.shape[-3]):
                    piece = ref[r] if len(ref.shape) == 3 else ref[half, r]
                    xs[r, pl.ds(begin, ROWS), :] = piece
        x = xs[...].reshape(-1, E)
        ks[...] = dot(x, kw_ref[...]).astype(BF16)
        vs[...] = dot(x, vw_ref[...]).astype(BF16)

    mine = pl.ds(pl.multiple_of(step * KEYS, KEYS), KEYS)
    cols = [slice(h * DH, (h + 1) * DH) for h in range(HEADS_DEV)]
    scores = [dot_nt(q_ref[:, c], ks[mine, c]) for c in cols]
    prob_grads = [dot_nt(g_ref[:, c], vs[mine, c]) for c in cols]
    lows, dscores = [], []
    for score, prob_grad in zip(scores, prob_grads):
        exponent = jnp.exp(score * SCALE)
        probs = exponent / jnp.sum(exponent, axis=-1, keepdims=True)
        delta = jnp.sum(probs * prob_grad, axis=-1, keepdims=True)
        lows.append(probs.astype(BF16))
        dscores.append((probs * (prob_grad - delta) * SCALE).astype(BF16))
    for c, low, dscore in zip(cols, lows, dscores):
        kgs[c, :] = dot_tn(q_ref[:, c], dscore).astype(BF16)
        vgs[c, :] = dot_tn(g_ref[:, c], low).astype(BF16)
    for c, low, dscore in zip(cols, lows, dscores):
        ctx_ref[:, c] = dot(low, vs[mine, c]).astype(BF16)
        qg_ref[:, c] = dot(dscore, ks[mine, c]).astype(BF16)
    backs[...] = (dot(kw_ref[...], kgs[...]) + dot(vw_ref[...], vgs[...])).astype(BF16)
    for shift in range(N_TP):
        begin = pl.multiple_of(member(shift) * EQ, 16)
        for k in range(KNB):
            outs[shift][k] = backs[pl.ds(begin, EQ), k * NTOK : (k + 1) * NTOK]


def attention(pieces, kw, vw, queries, ctx_grad, first, spans, held):
    whole = pl.BlockSpec((E, WIDTH), lambda c: (0, 0))
    span = pl.BlockSpec((SPAN, WIDTH), lambda c: (c + first, 0))
    back = pl.BlockSpec((KNB, EQ, NTOK), lambda c: (c, 0, 0))
    wide = jax.ShapeDtypeStruct((TOKENS_DEV, WIDTH), BF16)
    piece = jax.ShapeDtypeStruct((spans * KNB, EQ, NTOK), BF16)
    hops = len(pieces)
    return pl.pallas_call(
        functools.partial(attention_kernel, hops),
        grid=(spans,),
        out_shape=[wide, wide] + [piece] * N_TP,
        in_specs=[IN_VMEM] * hops + [whole, whole, span, span] + [ANYWHERE] * len(held),
        out_specs=[span, span] + [back] * N_TP,
        scratch_shapes=[
            pltpu.VMEM((spans * KNB, NTOK, E), BF16),
            pltpu.VMEM((spans * KEYS, WIDTH), BF16),
            pltpu.VMEM((spans * KEYS, WIDTH), BF16),
            pltpu.VMEM((WIDTH, KEYS), BF16),
            pltpu.VMEM((WIDTH, KEYS), BF16),
            pltpu.VMEM((E, KEYS), BF16),
        ],
        input_output_aliases={hops + 4 + i: i for i in range(len(held))},
        compiler_params=params(),
        cost_estimate=cost(spans * 2_200_000_000, 5_000_000 + spans * 1_500_000),
        name="attention",
    )(*pieces, kw, vw, queries, ctx_grad, *held)


def sum_kernel(*refs):
    out_ref = refs[-1]
    for r in range(out_ref.shape[0]):
        total = refs[0][r].astype(F32)
        for part in refs[1:-1]:
            total = total + part[r].astype(F32)
        out_ref[r] = total.astype(BF16)


def sum_parts(parts):
    return pl.pallas_call(
        sum_kernel,
        out_shape=jax.ShapeDtypeStruct(parts[0].shape, BF16),
        in_specs=[IN_VMEM] * len(parts),
        out_specs=IN_VMEM,
        compiler_params=params(),
        cost_estimate=cost(0, 2_000_000),
        name="sum_parts",
    )(*parts)


def place_kernel(neighbour_ref, sibling_neighbour_ref, *refs):
    grads, outs, table = refs[:4], refs[4:-1], refs[-1]
    half = GROUPS[0][1] * KNB
    for at in range(SLOTS):
        table[at] = REQ
    for whose, ref in enumerate((neighbour_ref, sibling_neighbour_ref)):
        for r, (away, other, slot) in enumerate(places_of(ref)):
            at = away * 2 * CAP + whose * CAP + slot

            @pl.when(other == 0)
            def _():
                table[at] = r

    for away in range(CHIPS):
        for block in range(2 * CAP):
            r = table[away * 2 * CAP + block]
            low, high = grads[2 * (block // CAP)], grads[2 * (block // CAP) + 1]
            out = outgoing(outs, away, block)

            @pl.when(r < half)
            def _():
                out[...] = low[r]

            @pl.when((r >= half) & (r < REQ))
            def _():
                out[...] = high[r - half]

            @pl.when(r >= REQ)
            def _():
                out[...] = jnp.zeros((EQ, NTOK), BF16)


def place(neighbour, sibling_neighbour, grads):
    return pl.pallas_call(
        place_kernel,
        out_shape=[jax.ShapeDtypeStruct((2 * CAP, EQ, NTOK), BF16)] * CHIPS,
        in_specs=[IN_SMEM, IN_SMEM] + [IN_VMEM] * len(grads),
        out_specs=[IN_VMEM] * CHIPS,
        scratch_shapes=[pltpu.SMEM((SLOTS,), jnp.int32)],
        compiler_params=params(),
        cost_estimate=cost(0, 3_000_000),
        name="place",
    )(neighbour, sibling_neighbour, *grads)


def collect_kernel(rows_ref, *refs):
    arrived, (out_ref, acc) = refs[:-2], refs[-2:]
    me = lax.axis_index("seq")
    chip, core = me // 2, lax.rem(me, 2)
    acc[...] = jnp.zeros(acc.shape, F32)
    for behind in range(CHIPS):
        device = lax.rem(chip - behind + CHIPS, CHIPS) * 2
        for block in range(2 * CAP):
            requester = device + (core if block < CAP else 1 - core)
            row = jnp.clip(rows_ref[requester, block % CAP], 0, STORED - 1)
            acc[row] += incoming(arrived, behind, block)[...].astype(F32)
    out_ref[...] = acc[...].astype(BF16)


def collect(rows, arrived):
    return pl.pallas_call(
        collect_kernel,
        out_shape=jax.ShapeDtypeStruct((STORED, EQ, NTOK), BF16),
        in_specs=[IN_SMEM] + [IN_VMEM] * len(arrived),
        out_specs=IN_VMEM,
        scratch_shapes=[pltpu.VMEM((STORED, EQ, NTOK), F32)],
        compiler_params=params(),
        cost_estimate=cost(0, 3_000_000),
        name="collect",
    )(rows, *arrived)


def swap(x):
    return lax.ppermute(x, "seq", [(i, i ^ 1) for i in range(N_SEQ)])


def ahead(x, by):
    return lax.ppermute(x, "seq", [(i, (i + 2 * by) % N_SEQ) for i in range(N_SEQ)])


def after(x, *done):
    return lax.optimization_barrier((x,) + done)[0]


def exchange_relayed(messages):
    local, right, *middle, left = messages
    right, left = ahead(right, 1), ahead(left, CHIPS - 1)
    middle = [ahead(x, by) for x, by in zip(middle, SENT[2:-1])]
    first = ahead(right[2 * CAP :], ACROSS - 1)
    second = ahead(left[2 * CAP :], ACROSS + 1)
    return [local, right, *middle, left, first, second]


def exchange(messages):
    arrived = [messages[0]] + [None] * (CHIPS - 1)
    for by, behind in ((3, 0), (5, 0), (4, 0), (2, 0), (6, 0), (1, 3), (7, 5)):
        message = messages[by]
        if behind:
            message = after(message, arrived[behind])
        arrived[by] = ahead(message, by)
    return arrived


def turn(x, by):
    return lax.ppermute(x, "tp", [(i, (i + by) % N_TP) for i in range(N_TP)])


def section_back(x):
    count = lax.axis_size("section")
    return lax.ppermute(x, "section", [(i, i - 1) for i in range(1, count)])


def deliver_kernel(*refs):
    out_ref = refs[-1]
    at = 0
    for ref in refs[:-1]:
        rows = ref.shape[0]
        out_ref[at : at + rows] = ref[...]
        at += rows


def deliver(parts):
    return pl.pallas_call(
        deliver_kernel,
        out_shape=jax.ShapeDtypeStruct((TOKENS_DEV, WIDTH), BF16),
        in_specs=[IN_VMEM] * len(parts),
        out_specs=IN_VMEM,
        compiler_params=params(),
        cost_estimate=cost(0, 2_000_000),
        name="deliver",
    )(*parts)


def body(queries, encoded, neighbour, send_rows, key_weight, value_weight, ctx_grad):
    sources, rows = neighbour[0], send_rows[0, 0]
    kw, vw = key_weight[0], value_weight[0]
    share = take_share(encoded[0])
    sibling_sources = swap(sources)
    sibling_rows = after(swap(rows), sibling_sources)
    arrived = exchange_relayed(pack_rows(rows, sibling_rows, share, swap(share)))
    picked = pick(sources, arrived)
    low, high = turn(picked[0], 1), turn(picked[0], -1)
    across = [turn(low[0], 1), turn(high[1], -1)]
    whole = [[picked[0], high] + across + [low]]
    own = after(picked[1], low, high, across[0])
    whole.append([own] + [turn(own, -shift) for shift in range(1, N_TP)])
    held = ()
    grads = []
    for group, (first, spans) in enumerate(GROUPS):
        *held, first_piece, second, third, fourth = attention(
            whole[group], kw, vw, queries[0], ctx_grad[0], first, spans, held
        )
        turned = [turn(x, by) for by, x in ((1, second), (2, third), (3, fourth))]
        grads.append(sum_parts([first_piece] + turned))
    context, query_grad = held
    passed = section_back(query_grad)
    messages = place(sources, sibling_sources, grads + [swap(grad) for grad in grads])
    messages = list(messages)
    messages[6] = after(messages[6], passed)
    returned = exchange(messages)
    encoded_grad = jnp.swapaxes(collect(rows, returned), 1, 2)
    passed = deliver([after(passed, returned[3])])
    return (context[None], passed[None], encoded_grad[None])


def solution(mesh):
    placed = (
        P("section", "seq", "tp"),
        P("section", "seq", None, None),
        P("section", "seq", None),
        P("section", "seq", None, None),
        P("section", None, "tp"),
        P("section", None, "tp"),
        P("section", "seq", "tp"),
    )
    return jax.shard_map(
        body,
        mesh=mesh,
        in_specs=placed,
        out_specs=(
            P("section", "seq", "tp"),
            P("section", "seq", "tp"),
            P("section", "seq", None, "tp"),
        ),
        check_vma=False,
    )
```
